32 devices in a mesh: row: 8 (over z, x), col: 4 (over y, core).
Axes of the slice: x: 2, y: 2, z: 4, core: 2. Of those that a mesh axis runs over, the one named last changes fastest.
Arguments:
- currents: bfloat16 [128, 64, 512], P('row', 'col'), may hold values from -6 to 6
- counts: int32 [128, 64], P('row', 'col'), may hold values from 0 to 16
- radiate: bfloat16 [512, 1024], replicated, may hold values from -0.25 to 0.25
- receive: bfloat16 [1024, 512], replicated, may hold values from -0.1875 to 0.1875
- near_blocks: bfloat16 [9, 512, 512], replicated, may hold values from -0.09375 to 0.09375
- translate: float32 [4, 49, 1024], replicated, may hold values from -0.84 to 0.84
- shift: float32 [3, 4, 1024], replicated, may hold values from -3 to 3
Outputs:
- field: bfloat16 [128, 64, 512], P('row', 'col')
The draws below stay inside these ranges and needn't reach their ends.
Inputs may be any that keep to these rules, and one draw needn't show every extreme that they name: `counts`: atoms present in each leaf box; they occupy its first slots.
All inputs are finite; a program needn't handle non-finite values.
Results may differ from the reference program's by a relative error of at most 0.017.
Values may be sent and summed in bfloat16 or wider, within the bound.
A program may use at most 192 MiB of HBM per device.

```python
import jax
import jax.numpy as jnp
from jax import lax

U = 16
SLOTS = 16
LEVELS = 4
W = 512
P_SIZE = 1024
NBX = 128
NBY = 64


def plant(result, key, least, high):
    extent = result.shape
    spot = [jax.random.randint(jax.random.fold_in(key, axis), (), 0, extent[axis]) for axis in range(len(extent))]
    result = result.at[tuple(spot)].set(least)
    longest = extent.index(max(extent))
    spot[longest] = (spot[longest] + 1) % extent[longest]
    return result.at[tuple(spot)].set(high)


def block_scale(key, shape, pieces, least, high):
    factor_of, own = 1.0, jax.random.fold_in(key, 6)
    for dim, parts in pieces:
        draws = jnp.exp(jax.random.uniform(jax.random.fold_in(own, dim), (parts,), jnp.float32, least / len(pieces), high / len(pieces)))
        factor_of = factor_of * jnp.repeat(draws, shape[dim] // parts).reshape([-1 if axis == dim else 1 for axis in range(len(shape))])
    return factor_of


def gaussian(stream_key, dims, scale, limit, cuts=(), kind=jnp.bfloat16):
    factor_of = block_scale(stream_key, dims, cuts, -0.22, 0.18) if cuts else 1.0
    array = jax.random.normal(stream_key, dims, jnp.float32) * scale * factor_of
    return jnp.minimum(jnp.maximum(array, -limit), limit).astype(kind)


def setup_inputs(seed: int = 0) -> dict:
    seeds = jax.random.split(jax.random.key(seed), 8)
    currents = gaussian(seeds[0], (NBX, NBY, W), 1.0, 6.0, ((0, 8), (1, 4)))
    counts = plant(jax.random.randint(seeds[1], (NBX, NBY), 0, SLOTS + 1), jax.random.fold_in(seeds[1], 1), 0, SLOTS).astype(jnp.int32)
    radiate = gaussian(seeds[2], (W, P_SIZE), W ** -0.5, 0.25)
    receive = gaussian(seeds[3], (P_SIZE, W), P_SIZE ** -0.5, 0.1875)
    near_blocks = gaussian(seeds[4], (9, W, W), (9 * W) ** -0.5, 0.09375)
    translate = gaussian(seeds[5], (LEVELS, 49, P_SIZE), 0.14, 0.84, (), jnp.float32)
    shift = gaussian(seeds[6], (LEVELS - 1, 4, P_SIZE), 0.5, 3.0, (), jnp.float32)
    return {"currents": currents, "counts": counts, "radiate": radiate, "receive": receive, "near_blocks": near_blocks, "translate": translate, "shift": shift}


def rotate(factors, pattern):
    samples = pattern.shape[-1] // 2
    t_re = factors[..., :samples]
    t_im = factors[..., samples:]
    p_re = pattern[..., :samples]
    p_im = pattern[..., samples:]
    return jnp.concatenate([t_re * p_re - t_im * p_im, t_re * p_im + t_im * p_re], axis=-1)


def rotate_back(factors, pattern):
    samples = pattern.shape[-1] // 2
    t_re = factors[..., :samples]
    t_im = factors[..., samples:]
    p_re = pattern[..., :samples]
    p_im = pattern[..., samples:]
    return jnp.concatenate([t_re * p_re + t_im * p_im, t_re * p_im - t_im * p_re], axis=-1)


def ascend(children, factors):
    size_x, size_y, last_dim = children.shape
    grouped = children.astype(jnp.float32).reshape(size_x // 2, 2, size_y // 2, 2, last_dim)
    summed = jnp.zeros((size_x // 2, size_y // 2, last_dim), jnp.float32)
    for bit_x in range(2):
        for bit_y in range(2):
            summed = summed + rotate(factors[2 * bit_x + bit_y], grouped[:, bit_x, :, bit_y])
    return summed.astype(jnp.bfloat16)


def descend(parent, factors):
    size_x, size_y, last_dim = parent.shape
    stacked = []
    for bit_x in range(2):
        siblings = [rotate_back(factors[2 * bit_x + bit_y], parent) for bit_y in range(2)]
        stacked.append(jnp.stack(siblings, axis=2))
    return jnp.stack(stacked, axis=1).reshape(2 * size_x, 2 * size_y, last_dim)


def far_field(padded, factors, size_x, size_y):
    index_x = jnp.arange(size_x, dtype=jnp.int32)
    index_y = jnp.arange(size_y, dtype=jnp.int32)
    summed = jnp.zeros((size_x, size_y, padded.shape[-1]), jnp.float32)
    for step_x in range(-3, 4):
        keep_x = jnp.abs((index_x + step_x) // 2 - index_x // 2) <= 1
        for step_y in range(-3, 4):
            if max(abs(step_x), abs(step_y)) < 2:
                continue
            keep_y = jnp.abs((index_y + step_y) // 2 - index_y // 2) <= 1
            keep_both = keep_x[:, None] & keep_y[None, :]
            source = padded[3 + step_x:3 + step_x + size_x, 3 + step_y:3 + step_y + size_y].astype(jnp.float32)
            contrib = rotate(factors[(step_x + 3) * 7 + step_y + 3], source)
            summed = summed + jnp.where(keep_both[:, :, None], contrib, 0.0)
    return summed


def reference(currents, counts, radiate, receive, near_blocks, translate, shift):
    size_x, size_y, unknowns = currents.shape
    slot_of = lax.broadcasted_iota(jnp.int32, (1, 1, unknowns), 2) // (2 * U)
    occupied = slot_of < counts[:, :, None]
    masked = jnp.where(occupied, currents, jnp.zeros_like(currents))
    padded_near = jnp.pad(masked, ((1, 1), (1, 1), (0, 0)))
    near_sum = jnp.zeros((size_x * size_y, unknowns), jnp.float32)
    for step_x in range(-1, 2):
        for step_y in range(-1, 2):
            source = padded_near[1 + step_x:1 + step_x + size_x, 1 + step_y:1 + step_y + size_y].reshape(size_x * size_y, unknowns)
            near_sum = near_sum + jnp.dot(source, near_blocks[(step_x + 1) * 3 + step_y + 1], preferred_element_type=jnp.float32)
    flat_rows = masked.reshape(size_x * size_y, unknowns)
    leaf_pattern = jnp.dot(flat_rows, radiate, preferred_element_type=jnp.float32).astype(jnp.bfloat16)
    pyramid = [leaf_pattern.reshape(size_x, size_y, P_SIZE)]
    for level_no in range(1, LEVELS):
        pyramid.append(ascend(pyramid[-1], shift[level_no - 1]))
    top_pattern = pyramid[LEVELS - 1]
    incoming = far_field(jnp.pad(top_pattern, ((3, 3), (3, 3), (0, 0))), translate[LEVELS - 1], top_pattern.shape[0], top_pattern.shape[1])
    for level_no in range(LEVELS - 2, -1, -1):
        current = pyramid[level_no]
        far_sum = far_field(jnp.pad(current, ((3, 3), (3, 3), (0, 0))), translate[level_no], current.shape[0], current.shape[1])
        incoming = far_sum + descend(incoming, shift[level_no])
    incoming_half = incoming.astype(jnp.bfloat16).reshape(size_x * size_y, P_SIZE)
    back_sum = jnp.dot(incoming_half, receive, preferred_element_type=jnp.float32)
    field = (near_sum + back_sum).reshape(size_x, size_y, unknowns)
    return jnp.where(occupied, field, 0.0).astype(jnp.bfloat16)
```

```python
import functools

import jax
import jax.numpy as jnp
import numpy as np
from jax import lax
from jax.experimental import pallas as pl
from jax.experimental.pallas import tpu as pltpu
from jax.sharding import PartitionSpec as P

MESH = pl.DeviceIdType.MESH
F32 = jnp.float32
BF16 = jnp.bfloat16
U = 16
LEVELS = 4
DIRS = [(-1, 0), (1, 0), (0, -1), (0, 1), (-1, -1), (-1, 1), (1, -1), (1, 1)]
SIZE = [32, 32, 32, 32, 16, 16, 16, 16]
OFF = [0, 32, 64, 96, 128, 144, 160, 176]
ROWS = 192
OPP = [1, 0, 3, 2, 7, 6, 5, 4]
SHIFTS = [-2, -1, 0, 1, 2, 3]


def edge(n, step):
    return [0, 1] if step < 0 else ([n - 2, n - 1] if step > 0 else list(range(n)))


def halo(n, step):
    return [-2, -1] if step < 0 else ([n, n + 1] if step > 0 else list(range(n)))


def boxes(d, sizes, pick):
    out = []
    for level, (nx, ny) in enumerate(sizes):
        for x in pick(nx, DIRS[d][0]):
            for y in pick(ny, DIRS[d][1]):
                out.append((level, x, y))
    return out


def message_rows(sizes):
    where = {}
    for d in range(8):
        for k, box in enumerate(boxes(d, sizes, halo)):
            where[box] = OFF[d] + k
    return where


def tables(nx, ny):
    sizes = [(nx >> l, ny >> l) for l in range(LEVELS)]
    own_rows = nx * ny

    def zeros(m, k):
        return np.zeros((m, k), np.float32)

    ex, ey = zeros(own_rows, nx), zeros(own_rows, ny)
    send0 = zeros(ROWS, own_rows)
    perm = zeros(own_rows, own_rows)
    for x in range(nx):
        for y in range(ny):
            ex[x * ny + y, x] = 1
            ey[x * ny + y, y] = 1
            row = (2 * (x % 2) + y % 2) * (own_rows // 4) + (x // 2) * (ny // 2) + y // 2
            perm[row, x * ny + y] = 1
    for d in range(8):
        for k, (_, x, y) in enumerate(boxes(d, sizes[:1], edge)):
            send0[OFF[d] + k, x * ny + y] = 1
    ext_rows = ny + 8
    ext_own, ext_got = zeros((nx + 4) * ext_rows, own_rows), zeros((nx + 4) * ext_rows, ROWS)
    got0 = message_rows(sizes[:1])
    for x in range(-2, nx + 2):
        for y in range(-2, ny + 2):
            row = (x + 2) * ext_rows + y + 3
            if 0 <= x < nx and 0 <= y < ny:
                ext_own[row, x * ny + y] = 1
            else:
                ext_got[row, got0[(0, x, y)]] = 1
    upper = sizes[1:]
    base, total = [], 0
    for a, b in upper:
        base.append(total)
        total += -(-a * b // 8) * 8
    stack = -(-total // 16) * 16

    def own(level, x, y):
        return base[level] + x * upper[level][1] + y

    splits = []
    for level in range(2):
        a, b = upper[level]
        child = -(-a * b // 16) * 16
        quarter = max(8, a * b // 4)
        split = zeros(4 * quarter, child)
        for x in range(a):
            for y in range(b):
                split[(2 * (x % 2) + y % 2) * quarter + (x // 2) * (b // 2) + y // 2, x * b + y] = 1
        splits.append(split)
    send1 = zeros(ROWS, stack)
    for d in range(8):
        for k, (level, x, y) in enumerate(boxes(d, upper, edge)):
            send1[OFF[d] + k, own(level, x, y)] = 1
    got1 = message_rows(upper)
    rows = [max(8, b) for _, b in upper]
    count = sum(6 * (a + 4) * r for (a, _), r in zip(upper, rows))
    up_own, up_got = zeros(count, stack), zeros(count, ROWS)
    at = 0
    for level, (a, b) in enumerate(upper):
        for s in SHIFTS:
            for x in range(-2, a + 2):
                for y in range(b):
                    yy = y + s if s < 3 else (y + 3 if y % 2 == 0 else y - 3)
                    row = at + (x + 2) * rows[level] + y
                    if 0 <= x < a and 0 <= yy < b:
                        up_own[row, own(level, x, yy)] = 1
                    else:
                        up_got[row, got1[(level, x, yy)]] = 1
            at += (a + 4) * rows[level]
    lifts = []
    for level in range(LEVELS - 1):
        a, b = sizes[level]
        r, rp = max(8, b), max(8, b // 2)
        lift = zeros(a * r, (a // 2) * rp)
        for x in range(a):
            for y in range(b):
                lift[x * r + y, (x // 2) * rp + y // 2] = 1
        lifts.append(np.concatenate([lift] * 3, axis=1))
    out = dict(ex=ex, ey=ey, send0=send0, perm=perm, ext_own=ext_own, ext_got=ext_got, split1=splits[0],
               split2=splits[1], send1=send1, up_own=up_own, up_got=up_got, lift0=lifts[0], lift1=lifts[1], lift2=lifts[2])
    return out, sizes


def dot(a, b):
    return jnp.dot(a, b, preferred_element_type=F32)


def body(names, sizes, *refs):
    n_in = len(names)
    hbm = dict(zip(names, refs[:n_in]))
    out_ref = refs[n_in]
    vm = dict(zip(names, refs[n_in + 1 : 2 * n_in + 1]))
    (x_own, cs, cr, gp, lown, ls, lr, e0, f0, ns, ps0, psl, inc0, inc1, inc2, inc3, lift0, lift1, lift2, near, cnt,
     in_sem, s_send, s_recv) = refs[2 * n_in + 1 :]
    nx, ny = sizes[0]
    own = nx * ny
    w = x_own.shape[1]
    feat = gp.shape[1]
    half = feat // 2
    tiles = half // 128
    row, col = lax.axis_index("row"), lax.axis_index("col")
    n_row, n_col = lax.axis_size("row"), lax.axis_size("col")

    loads = {name: pltpu.make_async_copy(hbm[name], vm[name], in_sem.at[k]) for k, name in enumerate(names)}
    for name in names:
        loads[name].start()

    cr[...] = jnp.zeros_like(cr)
    lr[...] = jnp.zeros_like(lr)

    there, ident = [], []
    for dr, dc in DIRS:
        r, c = row + dr, col + dc
        ok = (r >= 0) & (r < n_row) & (c >= 0) & (c < n_col)
        there.append(ok)
        ident.append((r, c))
    barrier = pltpu.get_barrier_semaphore()
    total = jnp.int32(0)
    for d in range(8):
        total = total + there[d].astype(jnp.int32)

        @pl.when(there[d])
        def _():
            pl.semaphore_signal(barrier, inc=1, device_id=ident[d], device_id_type=MESH)

    def copy(phase, src, dst, d, recv):
        o = OPP[d]
        slot = d if recv else o
        return pltpu.make_async_remote_copy(
            src_ref=src.at[pl.ds(OFF[d], SIZE[d])],
            dst_ref=dst.at[pl.ds(OFF[slot], SIZE[d])],
            send_sem=s_send.at[phase, d],
            recv_sem=s_recv.at[phase, slot],
            device_id=ident[d],
            device_id_type=MESH,
        )

    def each(act):
        for d in range(8):
            @pl.when(there[d])
            def _():
                act(d)

    for name in ("counts", "ex", "ey", "currents", "send0"):
        loads[name].wait()
    per_row = dot(vm["ex"][...], vm["counts"][...].astype(F32).astype(BF16)) * vm["ey"][...].astype(F32)
    cnt[...] = dot(per_row.astype(BF16), jnp.ones((ny, w), BF16))
    slot_of = (lax.broadcasted_iota(jnp.int32, (own, w), 1) // (2 * U)).astype(F32)
    occupied = slot_of < cnt[...]
    flat = vm["currents"][...].reshape(own, w)
    x_own[...] = jnp.where(occupied, flat.astype(F32), 0.0).astype(BF16)
    cs[...] = dot(vm["send0"][...], x_own[...]).astype(BF16)
    pl.semaphore_wait(barrier, total)
    each(lambda d: copy(0, cs, cr, d, False).start())

    loads["perm"].wait()
    loads["radiate"].wait()
    loads["shift"].wait()
    mixed = dot(vm["perm"][...], x_own[...]).astype(BF16)
    gp[...] = dot(mixed, vm["radiate"][...]).astype(BF16).astype(F32)
    shift = vm["shift"]
    quarter = own // 4

    def gather_up(source, level, rows):
        res, ims = [], []
        for t in range(tiles):
            lr_, li_ = slice(t * 128, t * 128 + 128), slice(half + t * 128, half + t * 128 + 128)
            re = jnp.zeros((rows, 128), F32)
            im = jnp.zeros((rows, 128), F32)
            for ab in range(4):
                tr, ti = shift[level, ab : ab + 1, lr_], shift[level, ab : ab + 1, li_]
                pr, pi = source[ab * rows : (ab + 1) * rows, lr_], source[ab * rows : (ab + 1) * rows, li_]
                re = re + (tr * pr - ti * pi)
                im = im + (tr * pi + ti * pr)
            res.append(re)
            ims.append(im)
        return jnp.concatenate(res + ims, axis=1)

    p1 = gather_up(gp, 0, quarter).astype(BF16)
    lown[0:quarter] = p1
    loads["split1"].wait()
    loads["split2"].wait()
    loads["send1"].wait()
    q2 = quarter // 4
    p2 = gather_up(dot(vm["split1"][...], p1), 1, q2).astype(BF16)
    lown[quarter : quarter + q2] = p2
    p3 = gather_up(dot(vm["split2"][...], p2), 2, 8)
    tail = lown.shape[0] - quarter - q2
    lown[quarter + q2 :] = jnp.concatenate([p3, jnp.zeros((tail - 8, feat), F32)], axis=0).astype(BF16)
    ls[...] = dot(vm["send1"][...], lown[...]).astype(BF16)
    each(lambda d: copy(1, ls, lr, d, False).start())

    loads["ext_own"].wait()
    loads["ext_got"].wait()
    each(lambda d: copy(0, cs, cr, d, True).wait_recv())
    ext = dot(vm["ext_own"][...], x_own[...]) + dot(vm["ext_got"][...], cr[...])
    ext_rows = ny + 8
    f0[...] = ext.reshape(nx + 4, ext_rows, w)
    step_rows = 4 * ext_rows

    def radiate_some(k, _):
        some = f0[pl.ds(k * 4, 4)].reshape(step_rows, w).astype(BF16)
        e0[pl.ds(k * 4, 4)] = dot(some, vm["radiate"][...]).astype(BF16).astype(F32).reshape(4, ext_rows, feat)
        return 0

    lax.fori_loop(0, (nx + 4) // 4, radiate_some, 0)

    even16 = (lax.broadcasted_iota(jnp.int32, (1, ny, 128), 1) % 2) == 0
    pairs = nx // 2 + 2

    def shifted(k, _):
        for c in range(feat // 128):
            lanes = slice(c * 128, c * 128 + 128)
            for par in range(2):
                x = k * 2 + par
                for n, s in enumerate(SHIFTS):
                    v = e0[pl.ds(x, 1), 3 + s : 3 + s + ny, lanes]
                    if s == 3:
                        v = jnp.where(even16, v, e0[pl.ds(x, 1), 0:ny, lanes])
                    ps0[pl.ds(n * pairs + k, 1), par, :, lanes] = v
        return 0

    lax.fori_loop(0, pairs, shifted, 0)

    for n in range(3):
        ns[n] = f0[1 : nx + 3, 2 + n : 2 + n + ny, :].astype(BF16)
    loads["near_blocks"].wait()
    for k in range(9):
        dx, dy = k // 3, k % 3
        part = dot(ns[dy, dx : dx + nx].reshape(own, w), vm["near_blocks"][k])
        near[...] = part if k == 0 else near[...] + part

    loads["up_own"].wait()
    loads["up_got"].wait()
    loads["translate"].wait()
    each(lambda d: copy(1, ls, lr, d, True).wait_recv())
    blocks = psl.shape[0] // 6

    def upper_some(k, _):
        rows = pl.ds(pl.multiple_of(k * 96, 96), 96)
        v = dot(vm["up_own"][rows, :], lown[...]) + dot(vm["up_got"][rows, :], lr[...])
        psl[pl.ds(k * 6, 6)] = v.reshape(6, 2, 8, feat)
        return 0

    lax.fori_loop(0, blocks, upper_some, 0)

    translate = vm["translate"]

    def far(level, src, base, inc, lifted):
        rows = src.shape[2]
        n_pairs = sizes[level][0] // 2
        npair = n_pairs + 2
        ni = min(4, n_pairs)
        even = (lax.broadcasted_iota(jnp.int32, (rows, 128), 0) % 2) == 0

        def step(it, _):
            t, h = lax.rem(it, tiles), lax.div(it, tiles)
            rl = pl.ds(pl.multiple_of(t * 128, 128), 128)
            il = pl.ds(pl.multiple_of(half + t * 128, 128), 128)
            for a in range(2):
                re = jnp.zeros((ni, rows, 128), F32)
                im = jnp.zeros((ni, rows, 128), F32)
                for e in range(6):
                    dx = e - 2 - a
                    for n, s in enumerate(SHIFTS):
                        if max(abs(dx), abs(s)) < 2:
                            continue
                        k = (dx + 3) * 7 + s + 3
                        tr, ti = translate[level, k : k + 1, rl], translate[level, k : k + 1, il]
                        if s == 3:
                            m = (dx + 3) * 7
                            tr = jnp.where(even, tr, translate[level, m : m + 1, rl])
                            ti = jnp.where(even, ti, translate[level, m : m + 1, il])
                        at = pl.ds(base + n * npair + e // 2 + h * ni, ni)
                        pr, pi = src[at, e % 2, :, rl], src[at, e % 2, :, il]
                        re = re + (tr * pr - ti * pi)
                        im = im + (tr * pi + ti * pr)
                at = pl.ds(h * ni, ni)
                if lifted is not None:
                    tr = jnp.where(even, shift[level, 2 * a : 2 * a + 1, rl], shift[level, 2 * a + 1 : 2 * a + 2, rl])
                    ti = jnp.where(even, shift[level, 2 * a : 2 * a + 1, il], shift[level, 2 * a + 1 : 2 * a + 2, il])
                    pr, pi = lifted[at, a, :, rl], lifted[at, a, :, il]
                    re = re + (tr * pr + ti * pi)
                    im = im + (tr * pi - ti * pr)
                inc[at, a, :, rl] = re.astype(inc.dtype)
                inc[at, a, :, il] = im.astype(inc.dtype)
            return 0

        lax.fori_loop(0, tiles * (n_pairs // ni), step, 0)

    def lift(name, inc, dst):
        loads[name].wait()
        v = inc[...].reshape(-1, feat)
        hi = v.astype(BF16)
        rest = v - hi.astype(F32)
        mid = rest.astype(BF16)
        low = (rest - mid.astype(F32)).astype(BF16)
        dst[...] = dot(vm[name][...], jnp.concatenate([hi, mid, low], axis=0)).reshape(dst.shape)

    bases, at = [], 0
    for a, _ in sizes[1:]:
        bases.append(at)
        at += 6 * (a // 2 + 2)
    far(3, psl, bases[2], inc3, None)
    lift("lift2", inc3, lift2)
    far(2, psl, bases[1], inc2, lift2)
    lift("lift1", inc2, lift1)
    far(1, psl, bases[0], inc1, lift1)
    lift("lift0", inc1, lift0)
    far(0, ps0, 0, inc0, lift0)

    loads["receive"].wait()
    field = near[...] + dot(inc0[...].reshape(own, feat), vm["receive"][...])
    out_ref[...] = jnp.where(slot_of < cnt[...], field, 0.0).astype(BF16).reshape(nx, ny, w)

    each(lambda d: copy(0, cs, cr, d, False).wait_send())
    each(lambda d: copy(1, ls, lr, d, False).wait_send())


ORDER = ["counts", "ex", "ey", "currents", "send0", "perm", "radiate", "shift", "split1", "split2", "send1", "ext_own",
         "ext_got", "near_blocks", "up_own", "up_got", "translate", "lift2", "lift1", "lift0", "receive"]


def shards(currents, counts, radiate, receive, near_blocks, translate, shift):
    nx, ny, w = currents.shape
    feat = radiate.shape[1]
    consts, sizes = tables(nx, ny)
    ops = {k: jnp.asarray(v, BF16) for k, v in consts.items()}
    ops.update(currents=currents, counts=counts, radiate=radiate, receive=receive, near_blocks=near_blocks,
               translate=translate, shift=shift)
    args = [ops[k] for k in ORDER]
    own = nx * ny
    stack = consts["send1"].shape[1]
    rows = [max(8, b) for _, b in sizes]

    def level_buffer(level, dtype):
        return pltpu.VMEM((sizes[level][0] // 2, 2, rows[level], feat), dtype)

    scratch = [pltpu.VMEM(a.shape, a.dtype) for a in args]
    scratch += [
        pltpu.VMEM((own, w), BF16),
        pltpu.VMEM((ROWS, w), BF16),
        pltpu.VMEM((ROWS, w), BF16),
        pltpu.VMEM((own, feat), F32),
        pltpu.VMEM((stack, feat), BF16),
        pltpu.VMEM((ROWS, feat), BF16),
        pltpu.VMEM((ROWS, feat), BF16),
        pltpu.VMEM((nx + 4, ny + 8, feat), F32),
        pltpu.VMEM((nx + 4, ny + 8, w), F32),
        pltpu.VMEM((3, nx + 2, ny, w), BF16),
        pltpu.VMEM((6 * (nx // 2 + 2), 2, ny, feat), F32),
        pltpu.VMEM((consts["up_own"].shape[0] // 16, 2, 8, feat), F32),
        level_buffer(0, BF16), level_buffer(1, F32), level_buffer(2, F32), level_buffer(3, F32),
        level_buffer(0, F32), level_buffer(1, F32), level_buffer(2, F32),
        pltpu.VMEM((own, w), F32),
        pltpu.VMEM((own, w), F32),
        pltpu.SemaphoreType.DMA((len(args),)),
        pltpu.SemaphoreType.DMA((2, 8)),
        pltpu.SemaphoreType.DMA((2, 8)),
    ]
    return pl.pallas_call(
        functools.partial(body, ORDER, sizes),
        out_shape=jax.ShapeDtypeStruct(currents.shape, BF16),
        in_specs=[pl.BlockSpec(memory_space=pl.ANY)] * len(args),
        out_specs=pl.BlockSpec(memory_space=pltpu.VMEM),
        scratch_shapes=scratch,
        compiler_params=pltpu.CompilerParams(
            collective_id=0, has_side_effects=True, vmem_limit_bytes=58 * 1024 * 1024
        ),
        cost_estimate=pl.CostEstimate(flops=3_000_000_000, bytes_accessed=12_000_000, transcendentals=0),
    )(*args)


def solution(mesh):
    return jax.shard_map(
        shards,
        mesh=mesh,
        in_specs=(P("row", "col", None), P("row", "col"), P(), P(), P(), P(), P()),
        out_specs=P("row", "col", None),
        check_vma=False,
    )
```

```python
import functools

import jax
import jax.numpy as jnp
import numpy as np
from jax import lax
from jax.experimental import pallas as pl
from jax.experimental.pallas import tpu as pltpu
from jax.sharding import PartitionSpec as P

MESH = pl.DeviceIdType.MESH
F32 = jnp.float32
BF16 = jnp.bfloat16
U = 16
LEVELS = 4
DIRS = [(-1, 0), (1, 0), (0, -1), (0, 1), (-1, -1), (-1, 1), (1, -1), (1, 1)]
SIZE = [32, 32, 32, 32, 16, 16, 16, 16]
OFF = [0, 32, 64, 96, 128, 144, 160, 176]
ROWS = 192
OPP = [1, 0, 3, 2, 7, 6, 5, 4]
SHIFTS = [-2, -1, 0, 1, 2, 3]


def edge(n, step):
    return [0, 1] if step < 0 else ([n - 2, n - 1] if step > 0 else list(range(n)))


def halo(n, step):
    return [-2, -1] if step < 0 else ([n, n + 1] if step > 0 else list(range(n)))


def boxes(d, sizes, pick):
    out = []
    for level, (nx, ny) in enumerate(sizes):
        for x in pick(nx, DIRS[d][0]):
            for y in pick(ny, DIRS[d][1]):
                out.append((level, x, y))
    return out


def message_rows(sizes):
    where = {}
    for d in range(8):
        for k, box in enumerate(boxes(d, sizes, halo)):
            where[box] = OFF[d] + k
    return where


def tables(nx, ny):
    sizes = [(nx >> l, ny >> l) for l in range(LEVELS)]
    own_rows = nx * ny

    def zeros(m, k):
        return np.zeros((m, k), np.float32)

    ex, ey = zeros(own_rows, nx), zeros(own_rows, ny)
    send0 = zeros(ROWS, own_rows)
    perm = zeros(own_rows, own_rows)
    for x in range(nx):
        for y in range(ny):
            ex[x * ny + y, x] = 1
            ey[x * ny + y, y] = 1
            row = (2 * (x % 2) + y % 2) * (own_rows // 4) + (x // 2) * (ny // 2) + y // 2
            perm[row, x * ny + y] = 1
    for d in range(8):
        for k, (_, x, y) in enumerate(boxes(d, sizes[:1], edge)):
            send0[OFF[d] + k, x * ny + y] = 1
    ext_rows = ny + 8
    ext_own, ext_got = zeros((nx + 4) * ext_rows, own_rows), zeros((nx + 4) * ext_rows, ROWS)
    got0 = message_rows(sizes[:1])
    for x in range(-2, nx + 2):
        for y in range(-2, ny + 2):
            row = (x + 2) * ext_rows + y + 3
            if 0 <= x < nx and 0 <= y < ny:
                ext_own[row, x * ny + y] = 1
            else:
                ext_got[row, got0[(0, x, y)]] = 1
    upper = sizes[1:]
    base, total = [], 0
    for a, b in upper:
        base.append(total)
        total += -(-a * b // 8) * 8
    stack = -(-total // 16) * 16

    def own(level, x, y):
        return base[level] + x * upper[level][1] + y

    splits = []
    for level in range(2):
        a, b = upper[level]
        child = -(-a * b // 16) * 16
        quarter = max(8, a * b // 4)
        split = zeros(4 * quarter, child)
        for x in range(a):
            for y in range(b):
                split[(2 * (x % 2) + y % 2) * quarter + (x // 2) * (b // 2) + y // 2, x * b + y] = 1
        splits.append(split)
    send1 = zeros(ROWS, stack)
    for d in range(8):
        for k, (level, x, y) in enumerate(boxes(d, upper, edge)):
            send1[OFF[d] + k, own(level, x, y)] = 1
    got1 = message_rows(upper)
    rows = [max(8, b) for _, b in upper]
    count = sum(6 * (a + 4) * r for (a, _), r in zip(upper, rows))
    up_own, up_got = zeros(count, stack), zeros(count, ROWS)
    at = 0
    for level, (a, b) in enumerate(upper):
        for s in SHIFTS:
            for x in range(-2, a + 2):
                for y in range(b):
                    yy = y + s if s < 3 else (y + 3 if y % 2 == 0 else y - 3)
                    row = at + (x + 2) * rows[level] + y
                    if 0 <= x < a and 0 <= yy < b:
                        up_own[row, own(level, x, yy)] = 1
                    else:
                        up_got[row, got1[(level, x, yy)]] = 1
            at += (a + 4) * rows[level]
    lifts = []
    for level in range(LEVELS - 1):
        a, b = sizes[level]
        r, rp = max(8, b), max(8, b // 2)
        lift = zeros(a * r, (a // 2) * rp)
        for x in range(a):
            for y in range(b):
                lift[x * r + y, (x // 2) * rp + y // 2] = 1
        lifts.append(np.concatenate([lift] * 3, axis=1))
    out = dict(ex=ex, ey=ey, send0=send0, perm=perm, ext_own=ext_own, ext_got=ext_got, split1=splits[0],
               split2=splits[1], send1=send1, up_own=up_own, up_got=up_got, lift0=lifts[0], lift1=lifts[1], lift2=lifts[2])
    return out, sizes


def dot(a, b):
    return jnp.dot(a, b, preferred_element_type=F32)


def body(names, sizes, *refs):
    n_in = len(names)
    hbm = dict(zip(names, refs[:n_in]))
    out_ref = refs[n_in]
    vm = dict(zip(names, refs[n_in + 1 : 2 * n_in + 1]))
    (x_own, cs, cr, gp, lown, ls, lr, e0, f0, ns, ps0, psl, far0, inc0, inc1, inc2, inc3, lift0, lift1, lift2, near, cnt,
     in_sem, s_send, s_recv) = refs[2 * n_in + 1 :]
    nx, ny = sizes[0]
    own = nx * ny
    w = x_own.shape[1]
    feat = gp.shape[1]
    half = feat // 2
    tiles = half // 128
    row, col = lax.axis_index("row"), lax.axis_index("col")
    n_row, n_col = lax.axis_size("row"), lax.axis_size("col")

    loads = {name: pltpu.make_async_copy(hbm[name], vm[name], in_sem.at[k]) for k, name in enumerate(names)}
    cr[...] = jnp.zeros_like(cr)
    lr[...] = jnp.zeros_like(lr)

    there, ident = [], []
    for dr, dc in DIRS:
        r, c = row + dr, col + dc
        ok = (r >= 0) & (r < n_row) & (c >= 0) & (c < n_col)
        there.append(ok)
        ident.append((r, c))
    barrier = pltpu.get_barrier_semaphore()
    total = jnp.int32(0)
    for d in range(8):
        total = total + there[d].astype(jnp.int32)

        @pl.when(there[d])
        def _():
            pl.semaphore_signal(barrier, inc=1, device_id=ident[d], device_id_type=MESH)

    for name in names[:EARLY]:
        loads[name].start()

    def copy(phase, src, dst, d, recv):
        o = OPP[d]
        slot = d if recv else o
        return pltpu.make_async_remote_copy(
            src_ref=src.at[pl.ds(OFF[d], SIZE[d])],
            dst_ref=dst.at[pl.ds(OFF[slot], SIZE[d])],
            send_sem=s_send.at[phase, d],
            recv_sem=s_recv.at[phase, slot],
            device_id=ident[d],
            device_id_type=MESH,
        )

    def each(act):
        for d in range(8):
            @pl.when(there[d])
            def _():
                act(d)

    for name in ("counts", "ex", "ey", "currents", "send0"):
        loads[name].wait()
    per_row = dot(vm["ex"][...], vm["counts"][...].astype(F32).astype(BF16)) * vm["ey"][...].astype(F32)
    cnt[...] = dot(per_row.astype(BF16), jnp.ones((ny, w), BF16))
    slot_of = (lax.broadcasted_iota(jnp.int32, (own, w), 1) // (2 * U)).astype(F32)
    occupied = slot_of < cnt[...]
    flat = vm["currents"][...].reshape(own, w)
    x_own[...] = jnp.where(occupied, flat.astype(F32), 0.0).astype(BF16)
    cs[...] = dot(vm["send0"][...], x_own[...]).astype(BF16)
    pl.semaphore_wait(barrier, total)
    each(lambda d: copy(0, cs, cr, d, False).start())
    for name in names[EARLY:]:
        loads[name].start()

    loads["perm"].wait()
    loads["radiate"].wait()
    loads["shift"].wait()
    mixed = dot(vm["perm"][...], x_own[...]).astype(BF16)
    gp[...] = dot(mixed, vm["radiate"][...]).astype(BF16).astype(F32)
    shift = vm["shift"]
    quarter = own // 4

    def gather_up(source, level, rows):
        res, ims = [], []
        for t in range(tiles):
            lr_, li_ = slice(t * 128, t * 128 + 128), slice(half + t * 128, half + t * 128 + 128)
            re = jnp.zeros((rows, 128), F32)
            im = jnp.zeros((rows, 128), F32)
            for ab in range(4):
                tr, ti = shift[level, ab : ab + 1, lr_], shift[level, ab : ab + 1, li_]
                pr, pi = source[ab * rows : (ab + 1) * rows, lr_], source[ab * rows : (ab + 1) * rows, li_]
                re = re + (tr * pr - ti * pi)
                im = im + (tr * pi + ti * pr)
            res.append(re)
            ims.append(im)
        return jnp.concatenate(res + ims, axis=1)

    p1 = gather_up(gp, 0, quarter).astype(BF16)
    lown[0:quarter] = p1
    loads["split1"].wait()
    loads["split2"].wait()
    loads["send1"].wait()
    q2 = quarter // 4
    p2 = gather_up(dot(vm["split1"][...], p1), 1, q2).astype(BF16)
    lown[quarter : quarter + q2] = p2
    p3 = gather_up(dot(vm["split2"][...], p2), 2, 8)
    tail = lown.shape[0] - quarter - q2
    lown[quarter + q2 :] = jnp.concatenate([p3, jnp.zeros((tail - 8, feat), F32)], axis=0).astype(BF16)
    ls[...] = dot(vm["send1"][...], lown[...]).astype(BF16)
    each(lambda d: copy(1, ls, lr, d, False).start())

    loads["ext_own"].wait()
    loads["ext_got"].wait()
    each(lambda d: copy(0, cs, cr, d, True).wait_recv())
    ext = dot(vm["ext_own"][...], x_own[...]) + dot(vm["ext_got"][...], cr[...])
    ext_rows = ny + 8
    f0[...] = ext.reshape(nx + 4, ext_rows, w)
    step_rows = 4 * ext_rows

    def radiate_some(k, _):
        some = f0[pl.ds(k * 4, 4)].reshape(step_rows, w).astype(BF16)
        e0[pl.ds(k * 4, 4)] = dot(some, vm["radiate"][...]).astype(BF16).astype(F32).reshape(4, ext_rows, feat)
        return 0

    lax.fori_loop(0, (nx + 4) // 4, radiate_some, 0)

    even16 = (lax.broadcasted_iota(jnp.int32, (1, ny, 128), 1) % 2) == 0
    pairs = nx // 2 + 2

    def shifted(k, _):
        for c in range(feat // 128):
            lanes = slice(c * 128, c * 128 + 128)
            for par in range(2):
                x = k * 2 + par
                for n, s in enumerate(SHIFTS):
                    v = e0[pl.ds(x, 1), 3 + s : 3 + s + ny, lanes]
                    if s == 3:
                        v = jnp.where(even16, v, e0[pl.ds(x, 1), 0:ny, lanes])
                    ps0[pl.ds(n * pairs + k, 1), par, :, lanes] = v
        return 0

    lax.fori_loop(0, pairs, shifted, 0)

    for n in range(3):
        ns[n] = f0[1 : nx + 3, 2 + n : 2 + n + ny, :].astype(BF16)
    loads["near_blocks"].wait()
    views = [ns[k % 3, k // 3 : k // 3 + nx].reshape(own, w) for k in range(9)]
    near[...] = dot(jnp.concatenate(views, axis=1), vm["near_blocks"][...].reshape(9 * w, w))

    loads["translate"].wait()
    translate = vm["translate"]

    def far(level, src, base, inc, lifted):
        rows = src.shape[2]
        n_pairs = sizes[level][0] // 2
        npair = n_pairs + 2
        ni = min(4, n_pairs)
        even = (lax.broadcasted_iota(jnp.int32, (rows, 128), 0) % 2) == 0

        def step(it, _):
            t, h = lax.rem(it, tiles), lax.div(it, tiles)
            rl = pl.ds(pl.multiple_of(t * 128, 128), 128)
            il = pl.ds(pl.multiple_of(half + t * 128, 128), 128)
            for a in range(2):
                re = jnp.zeros((ni, rows, 128), F32)
                im = jnp.zeros((ni, rows, 128), F32)
                for e in range(6):
                    dx = e - 2 - a
                    for n, s in enumerate(SHIFTS):
                        if max(abs(dx), abs(s)) < 2:
                            continue
                        k = (dx + 3) * 7 + s + 3
                        tr, ti = translate[k, level : level + 1, rl], translate[k, level : level + 1, il]
                        if s == 3:
                            m = (dx + 3) * 7
                            tr = jnp.where(even, tr, translate[m, level : level + 1, rl])
                            ti = jnp.where(even, ti, translate[m, level : level + 1, il])
                        at = pl.ds(base + n * npair + e // 2 + h * ni, ni)
                        pr, pi = src[at, e % 2, :, rl], src[at, e % 2, :, il]
                        re = re + (tr * pr - ti * pi)
                        im = im + (tr * pi + ti * pr)
                at = pl.ds(h * ni, ni)
                if lifted is not None:
                    tr = jnp.where(even, shift[level, 2 * a : 2 * a + 1, rl], shift[level, 2 * a + 1 : 2 * a + 2, rl])
                    ti = jnp.where(even, shift[level, 2 * a : 2 * a + 1, il], shift[level, 2 * a + 1 : 2 * a + 2, il])
                    pr, pi = lifted[at, a, :, rl], lifted[at, a, :, il]
                    re = re + (tr * pr + ti * pi)
                    im = im + (tr * pi - ti * pr)
                inc[at, a, :, rl] = re.astype(inc.dtype)
                inc[at, a, :, il] = im.astype(inc.dtype)
            return 0

        lax.fori_loop(0, tiles * (n_pairs // ni), step, 0)

    def lift(name, inc, dst):
        loads[name].wait()
        v = inc[...].reshape(-1, feat)
        hi = v.astype(BF16)
        rest = v - hi.astype(F32)
        mid = rest.astype(BF16)
        low = (rest - mid.astype(F32)).astype(BF16)
        dst[...] = dot(vm[name][...], jnp.concatenate([hi, mid, low], axis=0)).reshape(dst.shape)

    far(0, ps0, 0, far0, None)

    loads["up_own"].wait()
    loads["up_got"].wait()
    each(lambda d: copy(1, ls, lr, d, True).wait_recv())
    blocks = psl.shape[0] // 6

    def upper_some(k, _):
        rows = pl.ds(pl.multiple_of(k * 96, 96), 96)
        v = dot(vm["up_own"][rows, :], lown[...]) + dot(vm["up_got"][rows, :], lr[...])
        psl[pl.ds(k * 6, 6)] = v.reshape(6, 2, 8, feat)
        return 0

    lax.fori_loop(0, blocks, upper_some, 0)

    bases, at = [], 0
    for a, _ in sizes[1:]:
        bases.append(at)
        at += 6 * (a // 2 + 2)
    far(3, psl, bases[2], inc3, None)
    lift("lift2", inc3, lift2)
    far(2, psl, bases[1], inc2, lift2)
    lift("lift1", inc2, lift1)
    far(1, psl, bases[0], inc1, lift1)
    lift("lift0", inc1, lift0)

    even = (lax.broadcasted_iota(jnp.int32, (ny, 128), 0) % 2) == 0

    def from_parents(t, _):
        rl = pl.ds(pl.multiple_of(t * 128, 128), 128)
        il = pl.ds(pl.multiple_of(half + t * 128, 128), 128)
        for a in range(2):
            tr = jnp.where(even, shift[0, 2 * a : 2 * a + 1, rl], shift[0, 2 * a + 1 : 2 * a + 2, rl])
            ti = jnp.where(even, shift[0, 2 * a : 2 * a + 1, il], shift[0, 2 * a + 1 : 2 * a + 2, il])
            pr, pi = lift0[:, a, :, rl], lift0[:, a, :, il]
            inc0[:, a, :, rl] = (far0[:, a, :, rl] + (tr * pr + ti * pi)).astype(BF16)
            inc0[:, a, :, il] = (far0[:, a, :, il] + (tr * pi - ti * pr)).astype(BF16)
        return 0

    lax.fori_loop(0, tiles, from_parents, 0)

    loads["receive"].wait()
    field = near[...] + dot(inc0[...].reshape(own, feat), vm["receive"][...])
    out_ref[...] = jnp.where(slot_of < cnt[...], field, 0.0).reshape(nx, ny, w)

    each(lambda d: copy(0, cs, cr, d, False).wait_send())
    each(lambda d: copy(1, ls, lr, d, False).wait_send())


EARLY = 11
ORDER = ["counts", "ex", "ey", "currents", "send0", "perm", "radiate", "shift", "split1", "split2", "send1", "ext_own",
         "ext_got", "near_blocks", "up_own", "up_got", "translate", "lift2", "lift1", "lift0", "receive"]


def shards(currents, counts, radiate, receive, near_blocks, translate, shift):
    nx, ny, w = currents.shape
    feat = radiate.shape[1]
    consts, sizes = tables(nx, ny)
    ops = {k: jnp.asarray(v, BF16) for k, v in consts.items()}
    ops.update(currents=currents, counts=counts, radiate=radiate, receive=receive, near_blocks=near_blocks,
               translate=jnp.transpose(translate, (1, 0, 2)), shift=shift)
    args = [ops[k] for k in ORDER]
    own = nx * ny
    stack = consts["send1"].shape[1]
    rows = [max(8, b) for _, b in sizes]

    def level_buffer(level, dtype):
        return pltpu.VMEM((sizes[level][0] // 2, 2, rows[level], feat), dtype)

    scratch = [pltpu.VMEM(a.shape, a.dtype) for a in args]
    scratch += [
        pltpu.VMEM((own, w), BF16),
        pltpu.VMEM((ROWS, w), BF16),
        pltpu.VMEM((ROWS, w), BF16),
        pltpu.VMEM((own, feat), F32),
        pltpu.VMEM((stack, feat), BF16),
        pltpu.VMEM((ROWS, feat), BF16),
        pltpu.VMEM((ROWS, feat), BF16),
        pltpu.VMEM((nx + 4, ny + 8, feat), F32),
        pltpu.VMEM((nx + 4, ny + 8, w), F32),
        pltpu.VMEM((3, nx + 2, ny, w), BF16),
        pltpu.VMEM((6 * (nx // 2 + 2), 2, ny, feat), F32),
        pltpu.VMEM((consts["up_own"].shape[0] // 16, 2, 8, feat), F32),
        level_buffer(0, F32), level_buffer(0, BF16), level_buffer(1, F32), level_buffer(2, F32), level_buffer(3, F32),
        level_buffer(0, F32), level_buffer(1, F32), level_buffer(2, F32),
        pltpu.VMEM((own, w), F32),
        pltpu.VMEM((own, w), F32),
        pltpu.SemaphoreType.DMA((len(args),)),
        pltpu.SemaphoreType.DMA((2, 8)),
        pltpu.SemaphoreType.DMA((2, 8)),
    ]
    return pl.pallas_call(
        functools.partial(body, ORDER, sizes),
        out_shape=jax.ShapeDtypeStruct(currents.shape, F32),
        in_specs=[pl.BlockSpec(memory_space=pl.ANY)] * len(args),
        out_specs=pl.BlockSpec(memory_space=pltpu.VMEM),
        scratch_shapes=scratch,
        compiler_params=pltpu.CompilerParams(
            collective_id=0, has_side_effects=True, vmem_limit_bytes=58 * 1024 * 1024
        ),
        cost_estimate=pl.CostEstimate(flops=3_000_000_000, bytes_accessed=12_000_000, transcendentals=0),
    )(*args).astype(BF16)


def solution(mesh):
    return jax.shard_map(
        shards,
        mesh=mesh,
        in_specs=(P("row", "col", None), P("row", "col"), P(), P(), P(), P(), P()),
        out_specs=P("row", "col", None),
        check_vma=False,
    )
```

```python
import functools

import jax
import jax.numpy as jnp
import numpy as np
from jax import lax
from jax.experimental import pallas as pl
from jax.experimental.pallas import tpu as pltpu
from jax.sharding import PartitionSpec as P

MESH = pl.DeviceIdType.MESH
F32 = jnp.float32
BF16 = jnp.bfloat16
U = 16
LEVELS = 4
DIRS = [(-1, 0), (1, 0), (0, -1), (0, 1), (-1, -1), (-1, 1), (1, -1), (1, 1)]
SIZE = [32, 32, 32, 32, 16, 16, 16, 16]
OFF = [0, 32, 64, 96, 128, 144, 160, 176]
ROWS = 192
OPP = [1, 0, 3, 2, 7, 6, 5, 4]
SHIFTS = [-2, -1, 0, 1, 2, 3]


def edge(n, step):
    return [0, 1] if step < 0 else ([n - 2, n - 1] if step > 0 else list(range(n)))


def halo(n, step):
    return [-2, -1] if step < 0 else ([n, n + 1] if step > 0 else list(range(n)))


def boxes(d, sizes, pick):
    out = []
    for level, (nx, ny) in enumerate(sizes):
        for x in pick(nx, DIRS[d][0]):
            for y in pick(ny, DIRS[d][1]):
                out.append((level, x, y))
    return out


def message_rows(sizes):
    where = {}
    for d in range(8):
        for k, box in enumerate(boxes(d, sizes, halo)):
            where[box] = OFF[d] + k
    return where


def tables(nx, ny):
    sizes = [(nx >> l, ny >> l) for l in range(LEVELS)]
    own_rows = nx * ny

    def zeros(m, k):
        return np.zeros((m, k), np.float32)

    ex, ey = zeros(own_rows, nx), zeros(own_rows, ny)
    send0 = zeros(ROWS, own_rows)
    perm = zeros(own_rows, own_rows)
    for x in range(nx):
        for y in range(ny):
            ex[x * ny + y, x] = 1
            ey[x * ny + y, y] = 1
            row = (2 * (x % 2) + y % 2) * (own_rows // 4) + (x // 2) * (ny // 2) + y // 2
            perm[row, x * ny + y] = 1
    for d in range(8):
        for k, (_, x, y) in enumerate(boxes(d, sizes[:1], edge)):
            send0[OFF[d] + k, x * ny + y] = 1
    ext_rows = ny + 8
    ext_own, ext_got = zeros((nx + 4) * ext_rows, own_rows), zeros((nx + 4) * ext_rows, ROWS)
    got0 = message_rows(sizes[:1])
    for x in range(-2, nx + 2):
        for y in range(-2, ny + 2):
            row = (x + 2) * ext_rows + y + 3
            if 0 <= x < nx and 0 <= y < ny:
                ext_own[row, x * ny + y] = 1
            else:
                ext_got[row, got0[(0, x, y)]] = 1
    upper = sizes[1:]
    base, total = [], 0
    for a, b in upper:
        base.append(total)
        total += -(-a * b // 8) * 8
    stack = -(-total // 16) * 16

    def own(level, x, y):
        return base[level] + x * upper[level][1] + y

    splits = []
    for level in range(2):
        a, b = upper[level]
        child = -(-a * b // 16) * 16
        quarter = max(8, a * b // 4)
        split = zeros(4 * quarter, child)
        for x in range(a):
            for y in range(b):
                split[(2 * (x % 2) + y % 2) * quarter + (x // 2) * (b // 2) + y // 2, x * b + y] = 1
        splits.append(split)
    send1 = zeros(ROWS, stack)
    for d in range(8):
        for k, (level, x, y) in enumerate(boxes(d, upper, edge)):
            send1[OFF[d] + k, own(level, x, y)] = 1
    got1 = message_rows(upper)
    rows = [max(8, b) for _, b in upper]
    count = sum(6 * (a + 4) * r for (a, _), r in zip(upper, rows))
    up_own, up_got = zeros(count, stack), zeros(count, ROWS)
    at = 0
    for level, (a, b) in enumerate(upper):
        for s in SHIFTS:
            for x in range(-2, a + 2):
                for y in range(b):
                    yy = y + s if s < 3 else (y + 3 if y % 2 == 0 else y - 3)
                    row = at + (x + 2) * rows[level] + y
                    if 0 <= x < a and 0 <= yy < b:
                        up_own[row, own(level, x, yy)] = 1
                    else:
                        up_got[row, got1[(level, x, yy)]] = 1
            at += (a + 4) * rows[level]
    lifts = []
    for level in range(LEVELS - 1):
        a, b = sizes[level]
        r, rp = max(8, b), max(8, b // 2)
        lift = zeros(a * r, (a // 2) * rp)
        for x in range(a):
            for y in range(b):
                lift[x * r + y, (x // 2) * rp + y // 2] = 1
        lifts.append(np.concatenate([lift] * 3, axis=1))
    out = dict(ex=ex, ey=ey, send0=send0, perm=perm, ext_own=ext_own, ext_got=ext_got, split1=splits[0],
               split2=splits[1], send1=send1, up_own=up_own, up_got=up_got, lift0=lifts[0], lift1=lifts[1], lift2=lifts[2])
    return out, sizes


def dot(a, b):
    return jnp.dot(a, b, preferred_element_type=F32)


def body(names, sizes, *refs):
    n_in = len(names)
    hbm = dict(zip(names, refs[:n_in]))
    out_ref = refs[n_in]
    vm = dict(zip(names, refs[n_in + 1 : 2 * n_in + 1]))
    (x_own, cs, cr, gp, lown, ls, lr, e0, f0, ns, ps0, psl, far0, inc0, inc1, inc2, inc3, lift0, lift1, lift2, near, cnt,
     in_sem, s_send, s_recv) = refs[2 * n_in + 1 :]
    nx, ny = sizes[0]
    own = nx * ny
    w = x_own.shape[1]
    feat = gp.shape[1]
    half = feat // 2
    tiles = half // 128
    row, col = lax.axis_index("row"), lax.axis_index("col")
    n_row, n_col = lax.axis_size("row"), lax.axis_size("col")

    loads = {name: pltpu.make_async_copy(hbm[name], vm[name], in_sem.at[k]) for k, name in enumerate(names)}
    cr[...] = jnp.zeros_like(cr)
    lr[...] = jnp.zeros_like(lr)

    there, ident = [], []
    for dr, dc in DIRS:
        r, c = row + dr, col + dc
        ok = (r >= 0) & (r < n_row) & (c >= 0) & (c < n_col)
        there.append(ok)
        ident.append((r, c))
    barrier = pltpu.get_barrier_semaphore()
    total = jnp.int32(0)
    for d in range(8):
        total = total + there[d].astype(jnp.int32)

        @pl.when(there[d])
        def _():
            pl.semaphore_signal(barrier, inc=1, device_id=ident[d], device_id_type=MESH)

    for name in names[:EARLY]:
        loads[name].start()

    def copy(phase, src, dst, d, recv):
        o = OPP[d]
        slot = d if recv else o
        return pltpu.make_async_remote_copy(
            src_ref=src.at[pl.ds(OFF[d], SIZE[d])],
            dst_ref=dst.at[pl.ds(OFF[slot], SIZE[d])],
            send_sem=s_send.at[phase, d],
            recv_sem=s_recv.at[phase, slot],
            device_id=ident[d],
            device_id_type=MESH,
        )

    def each(act):
        for d in range(8):
            @pl.when(there[d])
            def _():
                act(d)

    for name in ("counts", "ex", "ey", "currents", "send0"):
        loads[name].wait()
    per_row = dot(vm["ex"][...], vm["counts"][...].astype(F32).astype(BF16)) * vm["ey"][...].astype(F32)
    cnt[...] = dot(per_row.astype(BF16), jnp.ones((ny, w), BF16))
    slot_of = (lax.broadcasted_iota(jnp.int32, (own, w), 1) // (2 * U)).astype(F32)
    occupied = slot_of < cnt[...]
    flat = vm["currents"][...].reshape(own, w)
    x_own[...] = jnp.where(occupied, flat.astype(F32), 0.0).astype(BF16)
    cs[...] = dot(vm["send0"][...], x_own[...]).astype(BF16)
    pl.semaphore_wait(barrier, total)
    each(lambda d: copy(0, cs, cr, d, False).start())
    for name in names[EARLY:]:
        loads[name].start()

    loads["perm"].wait()
    loads["radiate"].wait()
    loads["shift"].wait()
    mixed = dot(vm["perm"][...], x_own[...]).astype(BF16)
    gp[...] = dot(mixed, vm["radiate"][...]).astype(BF16).astype(F32)
    shift = vm["shift"]
    quarter = own // 4

    def gather_up(source, level, rows):
        res, ims = [], []
        for t in range(tiles):
            lr_, li_ = slice(t * 128, t * 128 + 128), slice(half + t * 128, half + t * 128 + 128)
            re = jnp.zeros((rows, 128), F32)
            im = jnp.zeros((rows, 128), F32)
            for ab in range(4):
                tr, ti = shift[level, ab : ab + 1, lr_], shift[level, ab : ab + 1, li_]
                pr, pi = source[ab * rows : (ab + 1) * rows, lr_], source[ab * rows : (ab + 1) * rows, li_]
                re = re + (tr * pr - ti * pi)
                im = im + (tr * pi + ti * pr)
            res.append(re)
            ims.append(im)
        return jnp.concatenate(res + ims, axis=1)

    p1 = gather_up(gp, 0, quarter).astype(BF16)
    lown[0:quarter] = p1
    loads["split1"].wait()
    loads["split2"].wait()
    loads["send1"].wait()
    q2 = quarter // 4
    p2 = gather_up(dot(vm["split1"][...], p1), 1, q2).astype(BF16)
    lown[quarter : quarter + q2] = p2
    p3 = gather_up(dot(vm["split2"][...], p2), 2, 8)
    tail = lown.shape[0] - quarter - q2
    lown[quarter + q2 :] = jnp.concatenate([p3, jnp.zeros((tail - 8, feat), F32)], axis=0).astype(BF16)
    ls[...] = dot(vm["send1"][...], lown[...]).astype(BF16)
    each(lambda d: copy(1, ls, lr, d, False).start())

    loads["ext_own"].wait()
    loads["ext_got"].wait()
    each(lambda d: copy(0, cs, cr, d, True).wait_recv())
    ext = dot(vm["ext_own"][...], x_own[...]) + dot(vm["ext_got"][...], cr[...])
    ext_rows = ny + 8
    for c in range(w // 128):
        f0[c] = ext[:, c * 128 : c * 128 + 128].reshape(nx + 4, ext_rows, 128)
    ext = ext.astype(BF16)
    for c in range(0, feat // 128, 2):
        pat = dot(ext, vm["radiate"][:, c * 128 : c * 128 + 256]).astype(BF16).astype(F32)
        e0[c] = pat[:, :128].reshape(nx + 4, ext_rows, 128)
        e0[c + 1] = pat[:, 128:].reshape(nx + 4, ext_rows, 128)

    even16 = (lax.broadcasted_iota(jnp.int32, (1, ny, 128), 1) % 2) == 0
    pairs = nx // 2 + 2

    def shifted(k, _):
        for c in range(feat // 128):
            lanes = slice(c * 128, c * 128 + 128)
            for par in range(2):
                x = k * 2 + par
                for n, s in enumerate(SHIFTS):
                    v = e0[c, pl.ds(x, 1), 3 + s : 3 + s + ny, :]
                    if s == 3:
                        v = jnp.where(even16, v, e0[c, pl.ds(x, 1), 0:ny, :])
                    ps0[pl.ds(n * pairs + k, 1), par, :, lanes] = v
        return 0

    lax.fori_loop(0, pairs, shifted, 0)

    for n in range(3):
        for c in range(w // 128):
            ns[n, :, :, c * 128 : c * 128 + 128] = f0[c, 1 : nx + 3, 2 + n : 2 + n + ny, :].astype(BF16)
    loads["near_blocks"].wait()
    views = [ns[k % 3, k // 3 : k // 3 + nx].reshape(own, w) for k in range(9)]
    near[...] = dot(jnp.concatenate(views, axis=1), vm["near_blocks"][...].reshape(9 * w, w))

    loads["translate"].wait()
    translate = vm["translate"]

    def far(level, src, base, inc, lifted):
        rows = src.shape[2]
        n_pairs = sizes[level][0] // 2
        npair = n_pairs + 2
        ni = min(4, n_pairs)
        even = (lax.broadcasted_iota(jnp.int32, (rows, 128), 0) % 2) == 0

        def step(it, _):
            t, h = lax.rem(it, tiles), lax.div(it, tiles)
            rl = pl.ds(pl.multiple_of(t * 128, 128), 128)
            il = pl.ds(pl.multiple_of(half + t * 128, 128), 128)
            for a in range(2):
                re = jnp.zeros((ni, rows, 128), F32)
                im = jnp.zeros((ni, rows, 128), F32)
                for e in range(6):
                    dx = e - 2 - a
                    for n, s in enumerate(SHIFTS):
                        if max(abs(dx), abs(s)) < 2:
                            continue
                        k = (dx + 3) * 7 + s + 3
                        tr, ti = translate[k, level : level + 1, rl], translate[k, level : level + 1, il]
                        if s == 3:
                            m = (dx + 3) * 7
                            tr = jnp.where(even, tr, translate[m, level : level + 1, rl])
                            ti = jnp.where(even, ti, translate[m, level : level + 1, il])
                        at = pl.ds(base + n * npair + e // 2 + h * ni, ni)
                        pr, pi = src[at, e % 2, :, rl], src[at, e % 2, :, il]
                        re = re + (tr * pr - ti * pi)
                        im = im + (tr * pi + ti * pr)
                at = pl.ds(h * ni, ni)
                if lifted is not None:
                    tr = jnp.where(even, shift[level, 2 * a : 2 * a + 1, rl], shift[level, 2 * a + 1 : 2 * a + 2, rl])
                    ti = jnp.where(even, shift[level, 2 * a : 2 * a + 1, il], shift[level, 2 * a + 1 : 2 * a + 2, il])
                    pr, pi = lifted[at, a, :, rl], lifted[at, a, :, il]
                    re = re + (tr * pr + ti * pi)
                    im = im + (tr * pi - ti * pr)
                inc[at, a, :, rl] = re.astype(inc.dtype)
                inc[at, a, :, il] = im.astype(inc.dtype)
            return 0

        lax.fori_loop(0, tiles * (n_pairs // ni), step, 0)

    def lift(name, inc, dst):
        loads[name].wait()
        v = inc[...].reshape(-1, feat)
        hi = v.astype(BF16)
        rest = v - hi.astype(F32)
        mid = rest.astype(BF16)
        low = (rest - mid.astype(F32)).astype(BF16)
        dst[...] = dot(vm[name][...], jnp.concatenate([hi, mid, low], axis=0)).reshape(dst.shape)

    far(0, ps0, 0, far0, None)

    loads["up_own"].wait()
    loads["up_got"].wait()
    each(lambda d: copy(1, ls, lr, d, True).wait_recv())
    for c in range(0, feat, 256):
        v = dot(vm["up_own"][...], lown[:, c : c + 256]) + dot(vm["up_got"][...], lr[:, c : c + 256])
        psl[:, :, :, c : c + 256] = v.reshape(psl.shape[0], 2, 8, 256)

    bases, at = [], 0
    for a, _ in sizes[1:]:
        bases.append(at)
        at += 6 * (a // 2 + 2)
    far(3, psl, bases[2], inc3, None)
    lift("lift2", inc3, lift2)
    far(2, psl, bases[1], inc2, lift2)
    lift("lift1", inc2, lift1)
    far(1, psl, bases[0], inc1, lift1)
    lift("lift0", inc1, lift0)

    even = (lax.broadcasted_iota(jnp.int32, (ny, 128), 0) % 2) == 0

    def from_parents(t, _):
        rl = pl.ds(pl.multiple_of(t * 128, 128), 128)
        il = pl.ds(pl.multiple_of(half + t * 128, 128), 128)
        for a in range(2):
            tr = jnp.where(even, shift[0, 2 * a : 2 * a + 1, rl], shift[0, 2 * a + 1 : 2 * a + 2, rl])
            ti = jnp.where(even, shift[0, 2 * a : 2 * a + 1, il], shift[0, 2 * a + 1 : 2 * a + 2, il])
            pr, pi = lift0[:, a, :, rl], lift0[:, a, :, il]
            inc0[:, a, :, rl] = (far0[:, a, :, rl] + (tr * pr + ti * pi)).astype(BF16)
            inc0[:, a, :, il] = (far0[:, a, :, il] + (tr * pi - ti * pr)).astype(BF16)
        return 0

    lax.fori_loop(0, tiles, from_parents, 0)

    loads["receive"].wait()
    field = near[...] + dot(inc0[...].reshape(own, feat), vm["receive"][...])
    out_ref[...] = jnp.where(slot_of < cnt[...], field, 0.0).astype(BF16).reshape(nx, ny, w)

    each(lambda d: copy(0, cs, cr, d, False).wait_send())
    each(lambda d: copy(1, ls, lr, d, False).wait_send())


def hand_over(src, dst, sem):
    copy = pltpu.make_async_copy(src, dst, sem)
    copy.start()
    copy.wait()


EARLY = 11
ORDER = ["counts", "ex", "ey", "currents", "send0", "perm", "radiate", "shift", "split1", "split2", "send1", "ext_own",
         "ext_got", "near_blocks", "up_own", "up_got", "translate", "lift2", "lift1", "lift0", "receive"]


def shards(currents, counts, radiate, receive, near_blocks, translate, shift):
    nx, ny, w = currents.shape
    feat = radiate.shape[1]
    consts, sizes = tables(nx, ny)
    ops = {k: jnp.asarray(v, BF16) for k, v in consts.items()}
    ops.update(currents=currents, counts=counts, radiate=radiate, receive=receive, near_blocks=near_blocks,
               translate=jnp.transpose(translate, (1, 0, 2)), shift=shift)
    args = [ops[k] for k in ORDER]
    own = nx * ny
    stack = consts["send1"].shape[1]
    rows = [max(8, b) for _, b in sizes]

    def level_buffer(level, dtype):
        return pltpu.VMEM((sizes[level][0] // 2, 2, rows[level], feat), dtype)

    scratch = [pltpu.VMEM(a.shape, a.dtype) for a in args]
    scratch += [
        pltpu.VMEM((own, w), BF16),
        pltpu.VMEM((ROWS, w), BF16),
        pltpu.VMEM((ROWS, w), BF16),
        pltpu.VMEM((own, feat), F32),
        pltpu.VMEM((stack, feat), BF16),
        pltpu.VMEM((ROWS, feat), BF16),
        pltpu.VMEM((ROWS, feat), BF16),
        pltpu.VMEM((feat // 128, nx + 4, ny + 8, 128), F32),
        pltpu.VMEM((w // 128, nx + 4, ny + 8, 128), F32),
        pltpu.VMEM((3, nx + 2, ny, w), BF16),
        pltpu.VMEM((6 * (nx // 2 + 2), 2, ny, feat), F32),
        pltpu.VMEM((consts["up_own"].shape[0] // 16, 2, 8, feat), F32),
        level_buffer(0, F32), level_buffer(0, BF16), level_buffer(1, F32), level_buffer(2, F32), level_buffer(3, F32),
        level_buffer(0, F32), level_buffer(1, F32), level_buffer(2, F32),
        pltpu.VMEM((own, w), F32),
        pltpu.VMEM((own, w), F32),
        pltpu.SemaphoreType.DMA((len(args),)),
        pltpu.SemaphoreType.DMA((2, 8)),
        pltpu.SemaphoreType.DMA((2, 8)),
    ]
    field = pl.pallas_call(
        functools.partial(body, ORDER, sizes),
        out_shape=jax.ShapeDtypeStruct(currents.shape, BF16),
        in_specs=[pl.BlockSpec(memory_space=pl.ANY)] * len(args),
        out_specs=pl.BlockSpec(memory_space=pltpu.VMEM),
        scratch_shapes=scratch,
        compiler_params=pltpu.CompilerParams(
            collective_id=0, has_side_effects=True, vmem_limit_bytes=58 * 1024 * 1024
        ),
        cost_estimate=pl.CostEstimate(flops=3_000_000_000, bytes_accessed=12_000_000, transcendentals=0),
    )(*args)
    return pl.pallas_call(
        hand_over,
        out_shape=jax.ShapeDtypeStruct(field.shape, field.dtype),
        in_specs=[pl.BlockSpec(memory_space=pl.ANY)],
        out_specs=pl.BlockSpec(memory_space=pl.ANY),
        scratch_shapes=[pltpu.SemaphoreType.DMA],
    )(field)


def solution(mesh):
    return jax.shard_map(
        shards,
        mesh=mesh,
        in_specs=(P("row", "col", None), P("row", "col"), P(), P(), P(), P(), P()),
        out_specs=P("row", "col", None),
        check_vma=False,
    )
```

```python
import functools

import jax
import jax.numpy as jnp
import numpy as np
from jax import lax
from jax.experimental import pallas as pl
from jax.experimental.pallas import tpu as pltpu
from jax.sharding import PartitionSpec as P

MESH = pl.DeviceIdType.MESH
F32 = jnp.float32
BF16 = jnp.bfloat16
U = 16
LEVELS = 4
DIRS = [(-1, 0), (1, 0), (0, -1), (0, 1), (-1, -1), (-1, 1), (1, -1), (1, 1)]
SIZE = [32, 32, 32, 32, 16, 16, 16, 16]
OFF = [0, 32, 64, 96, 128, 144, 160, 176]
ROWS = 192
OPP = [1, 0, 3, 2, 7, 6, 5, 4]
SHIFTS = [-2, -1, 0, 1, 2, 3]


def edge(n, step):
    return [0, 1] if step < 0 else ([n - 2, n - 1] if step > 0 else list(range(n)))


def halo(n, step):
    return [-2, -1] if step < 0 else ([n, n + 1] if step > 0 else list(range(n)))


def boxes(d, sizes, pick):
    out = []
    for level, (nx, ny) in enumerate(sizes):
        for x in pick(nx, DIRS[d][0]):
            for y in pick(ny, DIRS[d][1]):
                out.append((level, x, y))
    return out


def message_rows(sizes):
    where = {}
    for d in range(8):
        for k, box in enumerate(boxes(d, sizes, halo)):
            where[box] = OFF[d] + k
    return where


def tables(nx, ny):
    sizes = [(nx >> l, ny >> l) for l in range(LEVELS)]
    own_rows = nx * ny

    def zeros(m, k):
        return np.zeros((m, k), np.float32)

    ex, ey = zeros(own_rows, nx), zeros(own_rows, ny)
    send0 = zeros(ROWS, own_rows)
    perm = zeros(own_rows, own_rows)
    for x in range(nx):
        for y in range(ny):
            ex[x * ny + y, x] = 1
            ey[x * ny + y, y] = 1
            row = (2 * (x % 2) + y % 2) * (own_rows // 4) + (x // 2) * (ny // 2) + y // 2
            perm[row, x * ny + y] = 1
    for d in range(8):
        for k, (_, x, y) in enumerate(boxes(d, sizes[:1], edge)):
            send0[OFF[d] + k, x * ny + y] = 1
    ext_rows = ny + 8
    ext_own, ext_got = zeros((nx + 4) * ext_rows, own_rows), zeros((nx + 4) * ext_rows, ROWS)
    got0 = message_rows(sizes[:1])
    for x in range(-2, nx + 2):
        for y in range(-2, ny + 2):
            row = (x + 2) * ext_rows + y + 3
            if 0 <= x < nx and 0 <= y < ny:
                ext_own[row, x * ny + y] = 1
            else:
                ext_got[row, got0[(0, x, y)]] = 1
    upper = sizes[1:]
    base, total = [], 0
    for a, b in upper:
        base.append(total)
        total += -(-a * b // 8) * 8
    stack = -(-total // 16) * 16

    def own(level, x, y):
        return base[level] + x * upper[level][1] + y

    splits = []
    for level in range(2):
        a, b = upper[level]
        child = -(-a * b // 16) * 16
        quarter = max(8, a * b // 4)
        split = zeros(4 * quarter, child)
        for x in range(a):
            for y in range(b):
                split[(2 * (x % 2) + y % 2) * quarter + (x // 2) * (b // 2) + y // 2, x * b + y] = 1
        splits.append(split)
    send1 = zeros(ROWS, stack)
    for d in range(8):
        for k, (level, x, y) in enumerate(boxes(d, upper, edge)):
            send1[OFF[d] + k, own(level, x, y)] = 1
    got1 = message_rows(upper)
    rows = [max(8, b) for _, b in upper]
    count = sum(6 * (a + 4) * r for (a, _), r in zip(upper, rows))
    up_own, up_got = zeros(count, stack), zeros(count, ROWS)
    at = 0
    for level, (a, b) in enumerate(upper):
        for s in SHIFTS:
            for x in range(-2, a + 2):
                for y in range(b):
                    yy = y + s if s < 3 else (y + 3 if y % 2 == 0 else y - 3)
                    row = at + (x + 2) * rows[level] + y
                    if 0 <= x < a and 0 <= yy < b:
                        up_own[row, own(level, x, yy)] = 1
                    else:
                        up_got[row, got1[(level, x, yy)]] = 1
            at += (a + 4) * rows[level]
    lifts = []
    for level in range(LEVELS - 1):
        a, b = sizes[level]
        r, rp = max(8, b), max(8, b // 2)
        lift = zeros(a * r, (a // 2) * rp)
        for x in range(a):
            for y in range(b):
                lift[x * r + y, (x // 2) * rp + y // 2] = 1
        lifts.append(np.concatenate([lift] * 3, axis=1))
    out = dict(ex=ex, ey=ey, send0=send0, perm=perm, ext_own=ext_own, ext_got=ext_got, split1=splits[0],
               split2=splits[1], send1=send1, up_own=up_own, up_got=up_got, lift0=lifts[0], lift1=lifts[1], lift2=lifts[2])
    return out, sizes


def dot(a, b):
    return jnp.dot(a, b, preferred_element_type=F32)


def body(names, sizes, *refs):
    n_in = len(names)
    hbm = dict(zip(names, refs[:n_in]))
    out_ref = refs[n_in]
    vm = dict(zip(names, refs[n_in + 1 : 2 * n_in + 1]))
    (x_own, cs, cr, gp, lown, ls, lr, e0, f0, ns, ps0, psl, far0, inc0, inc1, inc2, inc3, lift0, lift1, lift2, near, cnt,
     in_sem, s_send, s_recv) = refs[2 * n_in + 1 :]
    nx, ny = sizes[0]
    own = nx * ny
    w = x_own.shape[1]
    feat = gp.shape[1]
    half = feat // 2
    tiles = half // 128
    row, col = lax.axis_index("row"), lax.axis_index("col")
    n_row, n_col = lax.axis_size("row"), lax.axis_size("col")

    loads = {name: pltpu.make_async_copy(hbm[name], vm[name], in_sem.at[k]) for k, name in enumerate(names)}
    cr[...] = jnp.zeros_like(cr)
    lr[...] = jnp.zeros_like(lr)

    there, ident = [], []
    for dr, dc in DIRS:
        r, c = row + dr, col + dc
        ok = (r >= 0) & (r < n_row) & (c >= 0) & (c < n_col)
        there.append(ok)
        ident.append((r, c))
    barrier = pltpu.get_barrier_semaphore()
    total = jnp.int32(0)
    for d in range(8):
        total = total + there[d].astype(jnp.int32)

        @pl.when(there[d])
        def _():
            pl.semaphore_signal(barrier, inc=1, device_id=ident[d], device_id_type=MESH)

    for name in names[:EARLY]:
        loads[name].start()

    def copy(phase, src, dst, d, recv):
        o = OPP[d]
        slot = d if recv else o
        return pltpu.make_async_remote_copy(
            src_ref=src.at[pl.ds(OFF[d], SIZE[d])],
            dst_ref=dst.at[pl.ds(OFF[slot], SIZE[d])],
            send_sem=s_send.at[phase, d],
            recv_sem=s_recv.at[phase, slot],
            device_id=ident[d],
            device_id_type=MESH,
        )

    def each(act):
        for d in range(8):
            @pl.when(there[d])
            def _():
                act(d)

    for name in ("counts", "ex", "ey", "currents", "send0"):
        loads[name].wait()
    per_row = dot(vm["ex"][...], vm["counts"][...].astype(F32).astype(BF16)) * vm["ey"][...].astype(F32)
    cnt[...] = dot(per_row.astype(BF16), jnp.ones((ny, w), BF16))
    slot_of = (lax.broadcasted_iota(jnp.int32, (own, w), 1) // (2 * U)).astype(F32)
    occupied = slot_of < cnt[...]
    flat = vm["currents"][...].reshape(own, w)
    x_own[...] = jnp.where(occupied, flat.astype(F32), 0.0).astype(BF16)
    cs[...] = dot(vm["send0"][...], x_own[...]).astype(BF16)
    pl.semaphore_wait(barrier, total)
    each(lambda d: copy(0, cs, cr, d, False).start())
    for name in names[EARLY:]:
        loads[name].start()

    loads["perm"].wait()
    loads["radiate"].wait()
    loads["shift"].wait()
    mixed = dot(vm["perm"][...], x_own[...]).astype(BF16)
    gp[...] = dot(mixed, vm["radiate"][...]).astype(BF16).astype(F32)
    shift = vm["shift"]
    quarter = own // 4

    def gather_up(source, level, rows):
        res, ims = [], []
        for t in range(tiles):
            lr_, li_ = slice(t * 128, t * 128 + 128), slice(half + t * 128, half + t * 128 + 128)
            re = jnp.zeros((rows, 128), F32)
            im = jnp.zeros((rows, 128), F32)
            for ab in range(4):
                tr, ti = shift[level, ab : ab + 1, lr_], shift[level, ab : ab + 1, li_]
                pr, pi = source[ab * rows : (ab + 1) * rows, lr_], source[ab * rows : (ab + 1) * rows, li_]
                re = re + (tr * pr - ti * pi)
                im = im + (tr * pi + ti * pr)
            res.append(re)
            ims.append(im)
        return jnp.concatenate(res + ims, axis=1)

    p1 = gather_up(gp, 0, quarter).astype(BF16)
    lown[0:quarter] = p1
    loads["split1"].wait()
    loads["split2"].wait()
    loads["send1"].wait()
    q2 = quarter // 4
    p2 = gather_up(dot(vm["split1"][...], p1), 1, q2).astype(BF16)
    lown[quarter : quarter + q2] = p2
    p3 = gather_up(dot(vm["split2"][...], p2), 2, 8)
    tail = lown.shape[0] - quarter - q2
    lown[quarter + q2 :] = jnp.concatenate([p3, jnp.zeros((tail - 8, feat), F32)], axis=0).astype(BF16)
    ls[...] = dot(vm["send1"][...], lown[...]).astype(BF16)
    each(lambda d: copy(1, ls, lr, d, False).start())

    loads["ext_own"].wait()
    loads["ext_got"].wait()
    each(lambda d: copy(0, cs, cr, d, True).wait_recv())
    ext = dot(vm["ext_own"][...], x_own[...]) + dot(vm["ext_got"][...], cr[...])
    ext_rows = ny + 8
    for c in range(w // 128):
        f0[c] = ext[:, c * 128 : c * 128 + 128].reshape(nx + 4, ext_rows, 128)
    ext = ext.astype(BF16)
    for c in range(0, feat // 128, 2):
        pat = dot(ext, vm["radiate"][:, c * 128 : c * 128 + 256]).astype(BF16).astype(F32)
        e0[c] = pat[:, :128].reshape(nx + 4, ext_rows, 128)
        e0[c + 1] = pat[:, 128:].reshape(nx + 4, ext_rows, 128)

    even16 = (lax.broadcasted_iota(jnp.int32, (1, ny, 128), 1) % 2) == 0
    pairs = nx // 2 + 2

    def shifted(k, _):
        for c in range(feat // 128):
            lanes = slice(c * 128, c * 128 + 128)
            for par in range(2):
                x = k * 2 + par
                for n, s in enumerate(SHIFTS):
                    v = e0[c, pl.ds(x, 1), 3 + s : 3 + s + ny, :]
                    if s == 3:
                        v = jnp.where(even16, v, e0[c, pl.ds(x, 1), 0:ny, :])
                    ps0[pl.ds(n * pairs + k, 1), par, :, lanes] = v.astype(BF16)
        return 0

    lax.fori_loop(0, pairs, shifted, 0)

    for n in range(3):
        for c in range(w // 128):
            ns[n, :, :, c * 128 : c * 128 + 128] = f0[c, 1 : nx + 3, 2 + n : 2 + n + ny, :].astype(BF16)
    loads["near_blocks"].wait()
    views = [ns[k % 3, k // 3 : k // 3 + nx].reshape(own, w) for k in range(9)]
    near[...] = dot(jnp.concatenate(views, axis=1), vm["near_blocks"][...].reshape(9 * w, w))

    loads["translate"].wait()
    translate = vm["translate"]

    def far(level, src, base, inc, lifted):
        rows = src.shape[2]
        n_pairs = sizes[level][0] // 2
        npair = n_pairs + 2
        ni = min(4, n_pairs)
        even = (lax.broadcasted_iota(jnp.int32, (rows, 128), 0) % 2) == 0

        def step(it, _):
            t, h = lax.rem(it, tiles), lax.div(it, tiles)
            rl = pl.ds(pl.multiple_of(t * 128, 128), 128)
            il = pl.ds(pl.multiple_of(half + t * 128, 128), 128)
            for a in range(2):
                re = jnp.zeros((ni, rows, 128), F32)
                im = jnp.zeros((ni, rows, 128), F32)
                narrow = src.dtype == BF16
                part, terms = None, 0
                for e in range(6):
                    dx = e - 2 - a
                    for n, s in enumerate(SHIFTS):
                        if max(abs(dx), abs(s)) < 2:
                            continue
                        k = (dx + 3) * 7 + s + 3
                        tr, ti = translate[k, level : level + 1, rl], translate[k, level : level + 1, il]
                        if s == 3:
                            m = (dx + 3) * 7
                            tr = jnp.where(even, tr, translate[m, level : level + 1, rl])
                            ti = jnp.where(even, ti, translate[m, level : level + 1, il])
                        at = pl.ds(base + n * npair + e // 2 + h * ni, ni)
                        pr, pi = src[at, e % 2, :, rl], src[at, e % 2, :, il]
                        if narrow:
                            tr = jnp.broadcast_to(tr, (rows, 128)).astype(BF16)
                            ti = jnp.broadcast_to(ti, (rows, 128)).astype(BF16)
                        more = (tr * pr - ti * pi, tr * pi + ti * pr)
                        part = more if part is None else (part[0] + more[0], part[1] + more[1])
                        terms += 1
                        if not narrow or terms % 3 == 0:
                            re = re + part[0].astype(F32)
                            im = im + part[1].astype(F32)
                            part = None
                at = pl.ds(h * ni, ni)
                if lifted is not None:
                    tr = jnp.where(even, shift[level, 2 * a : 2 * a + 1, rl], shift[level, 2 * a + 1 : 2 * a + 2, rl])
                    ti = jnp.where(even, shift[level, 2 * a : 2 * a + 1, il], shift[level, 2 * a + 1 : 2 * a + 2, il])
                    pr, pi = lifted[at, a, :, rl], lifted[at, a, :, il]
                    re = re + (tr * pr + ti * pi)
                    im = im + (tr * pi - ti * pr)
                inc[at, a, :, rl] = re.astype(inc.dtype)
                inc[at, a, :, il] = im.astype(inc.dtype)
            return 0

        lax.fori_loop(0, tiles * (n_pairs // ni), step, 0)

    def lift(name, inc, dst):
        loads[name].wait()
        v = inc[...].reshape(-1, feat)
        hi = v.astype(BF16)
        rest = v - hi.astype(F32)
        mid = rest.astype(BF16)
        low = (rest - mid.astype(F32)).astype(BF16)
        dst[...] = dot(vm[name][...], jnp.concatenate([hi, mid, low], axis=0)).reshape(dst.shape)

    far(0, ps0, 0, far0, None)

    loads["up_own"].wait()
    loads["up_got"].wait()
    each(lambda d: copy(1, ls, lr, d, True).wait_recv())
    for c in range(0, feat, 256):
        v = dot(vm["up_own"][...], lown[:, c : c + 256]) + dot(vm["up_got"][...], lr[:, c : c + 256])
        psl[:, :, :, c : c + 256] = v.reshape(psl.shape[0], 2, 8, 256)

    bases, at = [], 0
    for a, _ in sizes[1:]:
        bases.append(at)
        at += 6 * (a // 2 + 2)
    far(3, psl, bases[2], inc3, None)
    lift("lift2", inc3, lift2)
    far(2, psl, bases[1], inc2, lift2)
    lift("lift1", inc2, lift1)
    far(1, psl, bases[0], inc1, lift1)
    lift("lift0", inc1, lift0)

    even = (lax.broadcasted_iota(jnp.int32, (ny, 128), 0) % 2) == 0

    def from_parents(t, _):
        rl = pl.ds(pl.multiple_of(t * 128, 128), 128)
        il = pl.ds(pl.multiple_of(half + t * 128, 128), 128)
        for a in range(2):
            tr = jnp.where(even, shift[0, 2 * a : 2 * a + 1, rl], shift[0, 2 * a + 1 : 2 * a + 2, rl])
            ti = jnp.where(even, shift[0, 2 * a : 2 * a + 1, il], shift[0, 2 * a + 1 : 2 * a + 2, il])
            pr, pi = lift0[:, a, :, rl], lift0[:, a, :, il]
            inc0[:, a, :, rl] = (far0[:, a, :, rl] + (tr * pr + ti * pi)).astype(BF16)
            inc0[:, a, :, il] = (far0[:, a, :, il] + (tr * pi - ti * pr)).astype(BF16)
        return 0

    lax.fori_loop(0, tiles, from_parents, 0)

    loads["receive"].wait()
    field = near[...] + dot(inc0[...].reshape(own, feat), vm["receive"][...])
    out_ref[...] = jnp.where(slot_of < cnt[...], field, 0.0).astype(BF16).reshape(nx, ny, w)

    each(lambda d: copy(0, cs, cr, d, False).wait_send())
    each(lambda d: copy(1, ls, lr, d, False).wait_send())


def hand_over(src, dst):
    dst[...] = src[...]


EARLY = 11
ORDER = ["counts", "ex", "ey", "currents", "send0", "perm", "radiate", "shift", "split1", "split2", "send1", "ext_own",
         "ext_got", "near_blocks", "up_own", "up_got", "translate", "lift2", "lift1", "lift0", "receive"]


def shards(currents, counts, radiate, receive, near_blocks, translate, shift):
    nx, ny, w = currents.shape
    feat = radiate.shape[1]
    consts, sizes = tables(nx, ny)
    ops = {k: jnp.asarray(v, BF16) for k, v in consts.items()}
    ops.update(currents=currents, counts=counts, radiate=radiate, receive=receive, near_blocks=near_blocks,
               translate=jnp.transpose(translate, (1, 0, 2)), shift=shift)
    args = [ops[k] for k in ORDER]
    own = nx * ny
    stack = consts["send1"].shape[1]
    rows = [max(8, b) for _, b in sizes]

    def level_buffer(level, dtype):
        return pltpu.VMEM((sizes[level][0] // 2, 2, rows[level], feat), dtype)

    scratch = [pltpu.VMEM(a.shape, a.dtype) for a in args]
    scratch += [
        pltpu.VMEM((own, w), BF16),
        pltpu.VMEM((ROWS, w), BF16),
        pltpu.VMEM((ROWS, w), BF16),
        pltpu.VMEM((own, feat), F32),
        pltpu.VMEM((stack, feat), BF16),
        pltpu.VMEM((ROWS, feat), BF16),
        pltpu.VMEM((ROWS, feat), BF16),
        pltpu.VMEM((feat // 128, nx + 4, ny + 8, 128), F32),
        pltpu.VMEM((w // 128, nx + 4, ny + 8, 128), F32),
        pltpu.VMEM((3, nx + 2, ny, w), BF16),
        pltpu.VMEM((6 * (nx // 2 + 2), 2, ny, feat), BF16),
        pltpu.VMEM((consts["up_own"].shape[0] // 16, 2, 8, feat), F32),
        level_buffer(0, F32), level_buffer(0, BF16), level_buffer(1, F32), level_buffer(2, F32), level_buffer(3, F32),
        level_buffer(0, F32), level_buffer(1, F32), level_buffer(2, F32),
        pltpu.VMEM((own, w), F32),
        pltpu.VMEM((own, w), F32),
        pltpu.SemaphoreType.DMA((len(args),)),
        pltpu.SemaphoreType.DMA((2, 8)),
        pltpu.SemaphoreType.DMA((2, 8)),
    ]
    field = pl.pallas_call(
        functools.partial(body, ORDER, sizes),
        out_shape=jax.ShapeDtypeStruct(currents.shape, BF16),
        in_specs=[pl.BlockSpec(memory_space=pl.ANY)] * len(args),
        out_specs=pl.BlockSpec(memory_space=pltpu.VMEM),
        scratch_shapes=scratch,
        compiler_params=pltpu.CompilerParams(
            collective_id=0, has_side_effects=True, vmem_limit_bytes=58 * 1024 * 1024
        ),
        cost_estimate=pl.CostEstimate(flops=3_000_000_000, bytes_accessed=12_000_000, transcendentals=0),
    )(*args)
    return pl.pallas_call(
        hand_over,
        out_shape=jax.ShapeDtypeStruct(field.shape, field.dtype),
        in_specs=[pl.BlockSpec(memory_space=pltpu.VMEM)],
        out_specs=pl.BlockSpec(memory_space=pltpu.VMEM),
    )(field)


def solution(mesh):
    return jax.shard_map(
        shards,
        mesh=mesh,
        in_specs=(P("row", "col", None), P("row", "col"), P(), P(), P(), P(), P()),
        out_specs=P("row", "col", None),
        check_vma=False,
    )
```

```python
import functools

import jax
import jax.numpy as jnp
import numpy as np
from jax import lax
from jax.experimental import pallas as pl
from jax.experimental.pallas import tpu as pltpu
from jax.sharding import PartitionSpec as P

MESH = pl.DeviceIdType.MESH
F32 = jnp.float32
BF16 = jnp.bfloat16
U = 16
LEVELS = 4
DIRS = [(-1, 0), (1, 0), (0, -1), (0, 1), (-1, -1), (-1, 1), (1, -1), (1, 1)]
SIZE = [32, 32, 32, 32, 16, 16, 16, 16]
OFF = [0, 32, 64, 96, 128, 144, 160, 176]
ROWS = 192
OPP = [1, 0, 3, 2, 7, 6, 5, 4]
SHIFTS = [-2, -1, 0, 1, 2, 3]


def edge(n, step):
    return [0, 1] if step < 0 else ([n - 2, n - 1] if step > 0 else list(range(n)))


def halo(n, step):
    return [-2, -1] if step < 0 else ([n, n + 1] if step > 0 else list(range(n)))


def boxes(d, sizes, pick):
    out = []
    for level, (nx, ny) in enumerate(sizes):
        for x in pick(nx, DIRS[d][0]):
            for y in pick(ny, DIRS[d][1]):
                out.append((level, x, y))
    return out


def message_rows(sizes):
    where = {}
    for d in range(8):
        for k, box in enumerate(boxes(d, sizes, halo)):
            where[box] = OFF[d] + k
    return where


def tables(nx, ny):
    sizes = [(nx >> l, ny >> l) for l in range(LEVELS)]
    own_rows = nx * ny

    def zeros(m, k):
        return np.zeros((m, k), np.float32)

    ex, ey = zeros(own_rows, nx), zeros(own_rows, ny)
    send0 = zeros(ROWS, own_rows)
    perm = zeros(own_rows, own_rows)
    for x in range(nx):
        for y in range(ny):
            ex[x * ny + y, x] = 1
            ey[x * ny + y, y] = 1
            row = (2 * (x % 2) + y % 2) * (own_rows // 4) + (x // 2) * (ny // 2) + y // 2
            perm[row, x * ny + y] = 1
    for d in range(8):
        for k, (_, x, y) in enumerate(boxes(d, sizes[:1], edge)):
            send0[OFF[d] + k, x * ny + y] = 1
    ext_rows = ny + 8
    ext_own, ext_got = zeros((nx + 4) * ext_rows, own_rows), zeros((nx + 4) * ext_rows, ROWS)
    got0 = message_rows(sizes[:1])
    for x in range(-2, nx + 2):
        for y in range(-2, ny + 2):
            row = (x + 2) * ext_rows + y + 3
            if 0 <= x < nx and 0 <= y < ny:
                ext_own[row, x * ny + y] = 1
            else:
                ext_got[row, got0[(0, x, y)]] = 1
    upper = sizes[1:]
    base, total = [], 0
    for a, b in upper:
        base.append(total)
        total += -(-a * b // 8) * 8
    stack = -(-total // 16) * 16

    def own(level, x, y):
        return base[level] + x * upper[level][1] + y

    splits = []
    for level in range(2):
        a, b = upper[level]
        child = -(-a * b // 16) * 16
        quarter = max(8, a * b // 4)
        split = zeros(4 * quarter, child)
        for x in range(a):
            for y in range(b):
                split[(2 * (x % 2) + y % 2) * quarter + (x // 2) * (b // 2) + y // 2, x * b + y] = 1
        splits.append(split)
    send1 = zeros(ROWS, stack)
    for d in range(8):
        for k, (level, x, y) in enumerate(boxes(d, upper, edge)):
            send1[OFF[d] + k, own(level, x, y)] = 1
    got1 = message_rows(upper)
    rows = [max(8, b) for _, b in upper]
    count = sum(6 * (a + 4) * r for (a, _), r in zip(upper, rows))
    up_own, up_got = zeros(count, stack), zeros(count, ROWS)
    at = 0
    for level, (a, b) in enumerate(upper):
        for s in SHIFTS:
            for x in range(-2, a + 2):
                for y in range(b):
                    yy = y + s if s < 3 else (y + 3 if y % 2 == 0 else y - 3)
                    row = at + (x + 2) * rows[level] + y
                    if 0 <= x < a and 0 <= yy < b:
                        up_own[row, own(level, x, yy)] = 1
                    else:
                        up_got[row, got1[(level, x, yy)]] = 1
            at += (a + 4) * rows[level]
    lifts = []
    for level in range(LEVELS - 1):
        a, b = sizes[level]
        r, rp = max(8, b), max(8, b // 2)
        lift = zeros(a * r, (a // 2) * rp)
        for x in range(a):
            for y in range(b):
                lift[x * r + y, (x // 2) * rp + y // 2] = 1
        lifts.append(np.concatenate([lift] * 3, axis=1))
    out = dict(ex=ex, ey=ey, send0=send0, perm=perm, ext_own=ext_own, ext_got=ext_got, split1=splits[0],
               split2=splits[1], send1=send1, up_own=up_own, up_got=up_got, lift0=lifts[0], lift1=lifts[1], lift2=lifts[2])
    return out, sizes


def dot(a, b):
    return jnp.dot(a, b, preferred_element_type=F32)


def body(names, sizes, *refs):
    n_in = len(names)
    hbm = dict(zip(names, refs[:n_in]))
    out_ref = refs[n_in]
    vm = dict(zip(names, refs[n_in + 1 : 2 * n_in + 1]))
    (x_own, cs, cr, gp, lown, ls, lr, e0, f0, ns, ps0, psl, far0, inc0, inc1, inc2, inc3, lift0, lift1, lift2, near, cnt,
     in_sem, s_send, s_recv) = refs[2 * n_in + 1 :]
    nx, ny = sizes[0]
    own = nx * ny
    w = x_own.shape[1]
    feat = gp.shape[1]
    half = feat // 2
    tiles = half // 128
    row, col = lax.axis_index("row"), lax.axis_index("col")
    n_row, n_col = lax.axis_size("row"), lax.axis_size("col")

    loads = {name: pltpu.make_async_copy(hbm[name], vm[name], in_sem.at[k]) for k, name in enumerate(names)}
    cr[...] = jnp.zeros_like(cr)
    lr[...] = jnp.zeros_like(lr)

    there, ident = [], []
    for dr, dc in DIRS:
        r, c = row + dr, col + dc
        ok = (r >= 0) & (r < n_row) & (c >= 0) & (c < n_col)
        there.append(ok)
        ident.append((r, c))
    barrier = pltpu.get_barrier_semaphore()
    total = jnp.int32(0)
    for d in range(8):
        total = total + there[d].astype(jnp.int32)

        @pl.when(there[d])
        def _():
            pl.semaphore_signal(barrier, inc=1, device_id=ident[d], device_id_type=MESH)

    for name in names[:EARLY]:
        loads[name].start()

    def copy(phase, src, dst, d, recv):
        o = OPP[d]
        slot = d if recv else o
        return pltpu.make_async_remote_copy(
            src_ref=src.at[pl.ds(OFF[d], SIZE[d])],
            dst_ref=dst.at[pl.ds(OFF[slot], SIZE[d])],
            send_sem=s_send.at[phase, d],
            recv_sem=s_recv.at[phase, slot],
            device_id=ident[d],
            device_id_type=MESH,
        )

    def each(act):
        for d in range(8):
            @pl.when(there[d])
            def _():
                act(d)

    for name in ("counts", "ex", "ey", "currents", "send0"):
        loads[name].wait()
    per_row = dot(vm["ex"][...], vm["counts"][...].astype(F32).astype(BF16)) * vm["ey"][...].astype(F32)
    cnt[...] = dot(per_row.astype(BF16), jnp.ones((ny, w), BF16))
    slot_of = (lax.broadcasted_iota(jnp.int32, (own, w), 1) // (2 * U)).astype(F32)
    occupied = slot_of < cnt[...]
    flat = vm["currents"][...].reshape(own, w)
    x_own[...] = jnp.where(occupied, flat.astype(F32), 0.0).astype(BF16)
    cs[...] = dot(vm["send0"][...], x_own[...]).astype(BF16)
    pl.semaphore_wait(barrier, total)
    each(lambda d: copy(0, cs, cr, d, False).start())
    for name in names[EARLY:]:
        loads[name].start()

    loads["perm"].wait()
    loads["radiate"].wait()
    loads["shift"].wait()
    mixed = dot(vm["perm"][...], x_own[...]).astype(BF16)
    gp[...] = dot(mixed, vm["radiate"][...]).astype(BF16).astype(F32)
    shift = vm["shift"]
    quarter = own // 4

    def gather_up(source, level, rows):
        res, ims = [], []
        for t in range(tiles):
            lr_, li_ = slice(t * 128, t * 128 + 128), slice(half + t * 128, half + t * 128 + 128)
            re = jnp.zeros((rows, 128), F32)
            im = jnp.zeros((rows, 128), F32)
            for ab in range(4):
                tr, ti = shift[level, ab : ab + 1, lr_], shift[level, ab : ab + 1, li_]
                pr, pi = source[ab * rows : (ab + 1) * rows, lr_], source[ab * rows : (ab + 1) * rows, li_]
                re = re + (tr * pr - ti * pi)
                im = im + (tr * pi + ti * pr)
            res.append(re)
            ims.append(im)
        return jnp.concatenate(res + ims, axis=1)

    p1 = gather_up(gp, 0, quarter).astype(BF16)
    lown[0:quarter] = p1
    loads["split1"].wait()
    loads["split2"].wait()
    loads["send1"].wait()
    q2 = quarter // 4
    p2 = gather_up(dot(vm["split1"][...], p1), 1, q2).astype(BF16)
    lown[quarter : quarter + q2] = p2
    p3 = gather_up(dot(vm["split2"][...], p2), 2, 8)
    tail = lown.shape[0] - quarter - q2
    lown[quarter + q2 :] = jnp.concatenate([p3, jnp.zeros((tail - 8, feat), F32)], axis=0).astype(BF16)
    ls[...] = dot(vm["send1"][...], lown[...]).astype(BF16)
    each(lambda d: copy(1, ls, lr, d, False).start())

    loads["ext_own"].wait()
    loads["ext_got"].wait()
    each(lambda d: copy(0, cs, cr, d, True).wait_recv())
    ext = dot(vm["ext_own"][...], x_own[...]) + dot(vm["ext_got"][...], cr[...])
    ext_rows = ny + 8
    for c in range(w // 128):
        f0[c] = ext[:, c * 128 : c * 128 + 128].reshape(nx + 4, ext_rows, 128)
    ext = ext.astype(BF16)
    for c in range(0, feat // 128, 2):
        pat = dot(ext, vm["radiate"][:, c * 128 : c * 128 + 256]).astype(BF16).astype(F32)
        e0[c] = pat[:, :128].reshape(nx + 4, ext_rows, 128)
        e0[c + 1] = pat[:, 128:].reshape(nx + 4, ext_rows, 128)

    even16 = (lax.broadcasted_iota(jnp.int32, (1, ny, 128), 1) % 2) == 0
    pairs = nx // 2 + 2

    def shifted(k, _):
        for c in range(feat // 128):
            lanes = slice(c * 128, c * 128 + 128)
            for par in range(2):
                x = k * 2 + par
                for n, s in enumerate(SHIFTS):
                    v = e0[c, pl.ds(x, 1), 3 + s : 3 + s + ny, :]
                    if s == 3:
                        v = jnp.where(even16, v, e0[c, pl.ds(x, 1), 0:ny, :])
                    ps0[pl.ds(n * pairs + k, 1), par, :, lanes] = v.astype(BF16)
        return 0

    lax.fori_loop(0, pairs, shifted, 0)

    for n in range(3):
        for c in range(w // 128):
            ns[n, :, :, c * 128 : c * 128 + 128] = f0[c, 1 : nx + 3, 2 + n : 2 + n + ny, :].astype(BF16)
    loads["near_blocks"].wait()

    def near_part(n):
        columns = pl.ds(pl.multiple_of(n * (w // 2), w // 2), w // 2)
        views = [ns[k % 3, k // 3 : k // 3 + nx].reshape(own, w) for k in range(9)]
        near[:, columns] = dot(jnp.concatenate(views, axis=1), vm["near_blocks"][:, :, columns].reshape(9 * w, w // 2))

    loads["translate"].wait()
    translate = vm["translate"]

    def far(level, src, base, inc, lifted, beside=None):
        rows = src.shape[2]
        n_pairs = sizes[level][0] // 2
        npair = n_pairs + 2
        ni = min(4, n_pairs)
        even = (lax.broadcasted_iota(jnp.int32, (rows, 128), 0) % 2) == 0

        def step(it, _):
            if beside is None:
                piece(lax.rem(it, tiles), lax.div(it, tiles))
            else:
                beside(it)
                for k in range(tiles // 2):
                    for h in range(n_pairs // ni):
                        piece(it * (tiles // 2) + k, h)
            return 0

        def piece(t, h):
            rl = pl.ds(pl.multiple_of(t * 128, 128), 128)
            il = pl.ds(pl.multiple_of(half + t * 128, 128), 128)
            for a in range(2):
                re = jnp.zeros((ni, rows, 128), F32)
                im = jnp.zeros((ni, rows, 128), F32)
                narrow = src.dtype == BF16
                part, terms = None, 0
                for e in range(6):
                    dx = e - 2 - a
                    for n, s in enumerate(SHIFTS):
                        if max(abs(dx), abs(s)) < 2:
                            continue
                        k = (dx + 3) * 7 + s + 3
                        tr, ti = translate[k, level : level + 1, rl], translate[k, level : level + 1, il]
                        if s == 3:
                            m = (dx + 3) * 7
                            tr = jnp.where(even, tr, translate[m, level : level + 1, rl])
                            ti = jnp.where(even, ti, translate[m, level : level + 1, il])
                        at = pl.ds(base + n * npair + e // 2 + h * ni, ni)
                        pr, pi = src[at, e % 2, :, rl], src[at, e % 2, :, il]
                        if narrow:
                            tr = jnp.broadcast_to(tr, (rows, 128)).astype(BF16)
                            ti = jnp.broadcast_to(ti, (rows, 128)).astype(BF16)
                        more = (tr * pr - ti * pi, tr * pi + ti * pr)
                        part = more if part is None else (part[0] + more[0], part[1] + more[1])
                        terms += 1
                        if not narrow or terms % 3 == 0:
                            re = re + part[0].astype(F32)
                            im = im + part[1].astype(F32)
                            part = None
                at = pl.ds(h * ni, ni)
                if lifted is not None:
                    tr = jnp.where(even, shift[level, 2 * a : 2 * a + 1, rl], shift[level, 2 * a + 1 : 2 * a + 2, rl])
                    ti = jnp.where(even, shift[level, 2 * a : 2 * a + 1, il], shift[level, 2 * a + 1 : 2 * a + 2, il])
                    pr, pi = lifted[at, a, :, rl], lifted[at, a, :, il]
                    re = re + (tr * pr + ti * pi)
                    im = im + (tr * pi - ti * pr)
                inc[at, a, :, rl] = re.astype(inc.dtype)
                inc[at, a, :, il] = im.astype(inc.dtype)

        lax.fori_loop(0, tiles * (n_pairs // ni) if beside is None else 2, step, 0)

    def lift(name, inc, dst):
        loads[name].wait()
        v = inc[...].reshape(-1, feat)
        hi = v.astype(BF16)
        rest = v - hi.astype(F32)
        mid = rest.astype(BF16)
        low = (rest - mid.astype(F32)).astype(BF16)
        dst[...] = dot(vm[name][...], jnp.concatenate([hi, mid, low], axis=0)).reshape(dst.shape)

    far(0, ps0, 0, far0, None, near_part)

    loads["up_own"].wait()
    loads["up_got"].wait()
    each(lambda d: copy(1, ls, lr, d, True).wait_recv())
    for c in range(0, feat, 256):
        v = dot(vm["up_own"][...], lown[:, c : c + 256]) + dot(vm["up_got"][...], lr[:, c : c + 256])
        psl[:, :, :, c : c + 256] = v.reshape(psl.shape[0], 2, 8, 256)

    bases, at = [], 0
    for a, _ in sizes[1:]:
        bases.append(at)
        at += 6 * (a // 2 + 2)
    far(3, psl, bases[2], inc3, None)
    lift("lift2", inc3, lift2)
    far(2, psl, bases[1], inc2, lift2)
    lift("lift1", inc2, lift1)
    far(1, psl, bases[0], inc1, lift1)
    lift("lift0", inc1, lift0)

    even = (lax.broadcasted_iota(jnp.int32, (ny, 128), 0) % 2) == 0

    def from_parents(t, _):
        rl = pl.ds(pl.multiple_of(t * 128, 128), 128)
        il = pl.ds(pl.multiple_of(half + t * 128, 128), 128)
        for a in range(2):
            tr = jnp.where(even, shift[0, 2 * a : 2 * a + 1, rl], shift[0, 2 * a + 1 : 2 * a + 2, rl])
            ti = jnp.where(even, shift[0, 2 * a : 2 * a + 1, il], shift[0, 2 * a + 1 : 2 * a + 2, il])
            pr, pi = lift0[:, a, :, rl], lift0[:, a, :, il]
            inc0[:, a, :, rl] = (far0[:, a, :, rl] + (tr * pr + ti * pi)).astype(BF16)
            inc0[:, a, :, il] = (far0[:, a, :, il] + (tr * pi - ti * pr)).astype(BF16)
        return 0

    lax.fori_loop(0, tiles, from_parents, 0)

    loads["receive"].wait()
    field = near[...] + dot(inc0[...].reshape(own, feat), vm["receive"][...])
    out_ref[...] = jnp.where(slot_of < cnt[...], field, 0.0).astype(BF16).reshape(nx, ny, w)

    each(lambda d: copy(0, cs, cr, d, False).wait_send())
    each(lambda d: copy(1, ls, lr, d, False).wait_send())


def hand_over(src, dst):
    dst[...] = src[...]


EARLY = 11
ORDER = ["counts", "ex", "ey", "currents", "send0", "perm", "radiate", "shift", "split1", "split2", "send1", "ext_own",
         "ext_got", "near_blocks", "up_own", "up_got", "translate", "lift2", "lift1", "lift0", "receive"]


def shards(currents, counts, radiate, receive, near_blocks, translate, shift):
    nx, ny, w = currents.shape
    feat = radiate.shape[1]
    consts, sizes = tables(nx, ny)
    ops = {k: jnp.asarray(v, BF16) for k, v in consts.items()}
    ops.update(currents=currents, counts=counts, radiate=radiate, receive=receive, near_blocks=near_blocks,
               translate=jnp.transpose(translate, (1, 0, 2)), shift=shift)
    args = [ops[k] for k in ORDER]
    own = nx * ny
    stack = consts["send1"].shape[1]
    rows = [max(8, b) for _, b in sizes]

    def level_buffer(level, dtype):
        return pltpu.VMEM((sizes[level][0] // 2, 2, rows[level], feat), dtype)

    scratch = [pltpu.VMEM(a.shape, a.dtype) for a in args]
    scratch += [
        pltpu.VMEM((own, w), BF16),
        pltpu.VMEM((ROWS, w), BF16),
        pltpu.VMEM((ROWS, w), BF16),
        pltpu.VMEM((own, feat), F32),
        pltpu.VMEM((stack, feat), BF16),
        pltpu.VMEM((ROWS, feat), BF16),
        pltpu.VMEM((ROWS, feat), BF16),
        pltpu.VMEM((feat // 128, nx + 4, ny + 8, 128), F32),
        pltpu.VMEM((w // 128, nx + 4, ny + 8, 128), F32),
        pltpu.VMEM((3, nx + 2, ny, w), BF16),
        pltpu.VMEM((6 * (nx // 2 + 2), 2, ny, feat), BF16),
        pltpu.VMEM((consts["up_own"].shape[0] // 16, 2, 8, feat), F32),
        level_buffer(0, F32), level_buffer(0, BF16), level_buffer(1, F32), level_buffer(2, F32), level_buffer(3, F32),
        level_buffer(0, F32), level_buffer(1, F32), level_buffer(2, F32),
        pltpu.VMEM((own, w), F32),
        pltpu.VMEM((own, w), F32),
        pltpu.SemaphoreType.DMA((len(args),)),
        pltpu.SemaphoreType.DMA((2, 8)),
        pltpu.SemaphoreType.DMA((2, 8)),
    ]
    field = pl.pallas_call(
        functools.partial(body, ORDER, sizes),
        out_shape=jax.ShapeDtypeStruct(currents.shape, BF16),
        in_specs=[pl.BlockSpec(memory_space=pl.ANY)] * len(args),
        out_specs=pl.BlockSpec(memory_space=pltpu.VMEM),
        scratch_shapes=scratch,
        compiler_params=pltpu.CompilerParams(
            collective_id=0, has_side_effects=True, vmem_limit_bytes=58 * 1024 * 1024
        ),
        cost_estimate=pl.CostEstimate(flops=3_000_000_000, bytes_accessed=12_000_000, transcendentals=0),
    )(*args)
    return pl.pallas_call(
        hand_over,
        out_shape=jax.ShapeDtypeStruct(field.shape, field.dtype),
        in_specs=[pl.BlockSpec(memory_space=pltpu.VMEM)],
        out_specs=pl.BlockSpec(memory_space=pltpu.VMEM),
    )(field)


def solution(mesh):
    return jax.shard_map(
        shards,
        mesh=mesh,
        in_specs=(P("row", "col", None), P("row", "col"), P(), P(), P(), P(), P()),
        out_specs=P("row", "col", None),
        check_vma=False,
    )
```

```python
import functools

import jax
import jax.numpy as jnp
import numpy as np
from jax import lax
from jax.experimental import pallas as pl
from jax.experimental.pallas import tpu as pltpu
from jax.sharding import PartitionSpec as P

MESH = pl.DeviceIdType.MESH
F32 = jnp.float32
BF16 = jnp.bfloat16
U = 16
LEVELS = 4
DIRS = [(-1, 0), (1, 0), (0, -1), (0, 1), (-1, -1), (-1, 1), (1, -1), (1, 1)]
SIZE = [32, 32, 32, 32, 16, 16, 16, 16]
OFF = [0, 32, 64, 96, 128, 144, 160, 176]
ROWS = 192
OPP = [1, 0, 3, 2, 7, 6, 5, 4]
SHIFTS = [-2, -1, 0, 1, 2, 3]


def edge(n, step):
    return [0, 1] if step < 0 else ([n - 2, n - 1] if step > 0 else list(range(n)))


def halo(n, step):
    return [-2, -1] if step < 0 else ([n, n + 1] if step > 0 else list(range(n)))


def boxes(d, sizes, pick):
    out = []
    for level, (nx, ny) in enumerate(sizes):
        for x in pick(nx, DIRS[d][0]):
            for y in pick(ny, DIRS[d][1]):
                out.append((level, x, y))
    return out


def message_rows(sizes):
    where = {}
    for d in range(8):
        for k, box in enumerate(boxes(d, sizes, halo)):
            where[box] = OFF[d] + k
    return where


def tables(nx, ny):
    sizes = [(nx >> l, ny >> l) for l in range(LEVELS)]
    own_rows = nx * ny

    def zeros(m, k):
        return np.zeros((m, k), np.float32)

    ex, ey = zeros(own_rows, nx), zeros(own_rows, ny)
    send0 = zeros(ROWS, own_rows)
    perm = zeros(own_rows, own_rows)
    for x in range(nx):
        for y in range(ny):
            ex[x * ny + y, x] = 1
            ey[x * ny + y, y] = 1
            row = (2 * (x % 2) + y % 2) * (own_rows // 4) + (x // 2) * (ny // 2) + y // 2
            perm[row, x * ny + y] = 1
    for d in range(8):
        for k, (_, x, y) in enumerate(boxes(d, sizes[:1], edge)):
            send0[OFF[d] + k, x * ny + y] = 1
    ext_rows = ny + 8
    ext_own, ext_got = zeros((nx + 4) * ext_rows, own_rows), zeros((nx + 4) * ext_rows, ROWS)
    got0 = message_rows(sizes[:1])
    for x in range(-2, nx + 2):
        for y in range(-2, ny + 2):
            row = (x + 2) * ext_rows + y + 3
            if 0 <= x < nx and 0 <= y < ny:
                ext_own[row, x * ny + y] = 1
            else:
                ext_got[row, got0[(0, x, y)]] = 1
    upper = sizes[1:]
    base, total = [], 0
    for a, b in upper:
        base.append(total)
        total += -(-a * b // 8) * 8
    stack = -(-total // 16) * 16

    def own(level, x, y):
        return base[level] + x * upper[level][1] + y

    splits = []
    for level in range(2):
        a, b = upper[level]
        child = -(-a * b // 16) * 16
        quarter = max(8, a * b // 4)
        split = zeros(4 * quarter, child)
        for x in range(a):
            for y in range(b):
                split[(2 * (x % 2) + y % 2) * quarter + (x // 2) * (b // 2) + y // 2, x * b + y] = 1
        splits.append(split)
    send1 = zeros(ROWS, stack)
    for d in range(8):
        for k, (level, x, y) in enumerate(boxes(d, upper, edge)):
            send1[OFF[d] + k, own(level, x, y)] = 1
    got1 = message_rows(upper)
    rows = [max(8, b) for _, b in upper]
    count = sum(6 * (a + 4) * r for (a, _), r in zip(upper, rows))
    up_own, up_got = zeros(count, stack), zeros(count, ROWS)
    at = 0
    for level, (a, b) in enumerate(upper):
        for s in SHIFTS:
            for x in range(-2, a + 2):
                for y in range(b):
                    yy = y + s if s < 3 else (y + 3 if y % 2 == 0 else y - 3)
                    row = at + (x + 2) * rows[level] + y
                    if 0 <= x < a and 0 <= yy < b:
                        up_own[row, own(level, x, yy)] = 1
                    else:
                        up_got[row, got1[(level, x, yy)]] = 1
            at += (a + 4) * rows[level]
    lifts = []
    for level in range(LEVELS - 1):
        a, b = sizes[level]
        r, rp = max(8, b), max(8, b // 2)
        lift = zeros(a * r, (a // 2) * rp)
        for x in range(a):
            for y in range(b):
                lift[x * r + y, (x // 2) * rp + y // 2] = 1
        lifts.append(np.concatenate([lift] * 3, axis=1))
    out = dict(ex=ex, ey=ey, send0=send0, perm=perm, ext_own=ext_own, ext_got=ext_got, split1=splits[0],
               split2=splits[1], send1=send1, up_own=up_own, up_got=up_got, lift0=lifts[0], lift1=lifts[1], lift2=lifts[2])
    return out, sizes


def dot(a, b):
    return jnp.dot(a, b, preferred_element_type=F32)


def body(names, sizes, *refs):
    n_in = len(names)
    hbm = dict(zip(names, refs[:n_in]))
    out_ref = refs[n_in]
    vm = dict(zip(names, refs[n_in + 1 : 2 * n_in + 1]))
    (x_own, cs, cr, gp, lown, ls, lr, e0, f0, ns, ps0, psl, far0, inc0, inc1, inc2, inc3, lift0, lift1, lift2, near, cnt,
     in_sem, s_send, s_recv) = refs[2 * n_in + 1 :]
    nx, ny = sizes[0]
    own = nx * ny
    w = x_own.shape[1]
    feat = gp.shape[1]
    half = feat // 2
    tiles = half // 128
    row, col = lax.axis_index("row"), lax.axis_index("col")
    n_row, n_col = lax.axis_size("row"), lax.axis_size("col")

    loads = {name: pltpu.make_async_copy(hbm[name], vm[name], in_sem.at[k]) for k, name in enumerate(names)}
    cr[...] = jnp.zeros_like(cr)
    lr[...] = jnp.zeros_like(lr)

    there, ident = [], []
    for dr, dc in DIRS:
        r, c = row + dr, col + dc
        ok = (r >= 0) & (r < n_row) & (c >= 0) & (c < n_col)
        there.append(ok)
        ident.append((r, c))
    barrier = pltpu.get_barrier_semaphore()
    total = jnp.int32(0)
    for d in range(8):
        total = total + there[d].astype(jnp.int32)

        @pl.when(there[d])
        def _():
            pl.semaphore_signal(barrier, inc=1, device_id=ident[d], device_id_type=MESH)

    for name in names[:EARLY]:
        loads[name].start()

    def copy(phase, src, dst, d, recv):
        o = OPP[d]
        slot = d if recv else o
        return pltpu.make_async_remote_copy(
            src_ref=src.at[pl.ds(OFF[d], SIZE[d])],
            dst_ref=dst.at[pl.ds(OFF[slot], SIZE[d])],
            send_sem=s_send.at[phase, d],
            recv_sem=s_recv.at[phase, slot],
            device_id=ident[d],
            device_id_type=MESH,
        )

    def each(act):
        for d in range(8):
            @pl.when(there[d])
            def _():
                act(d)

    for name in ("counts", "ex", "ey", "currents", "send0"):
        loads[name].wait()
    per_row = dot(vm["ex"][...], vm["counts"][...].astype(F32).astype(BF16)) * vm["ey"][...].astype(F32)
    cnt[...] = dot(per_row.astype(BF16), jnp.ones((ny, w), BF16))
    slot_of = (lax.broadcasted_iota(jnp.int32, (own, w), 1) // (2 * U)).astype(F32)
    occupied = slot_of < cnt[...]
    flat = vm["currents"][...].reshape(own, w)
    x_own[...] = jnp.where(occupied, flat.astype(F32), 0.0).astype(BF16)
    cs[...] = dot(vm["send0"][...], x_own[...]).astype(BF16)
    pl.semaphore_wait(barrier, total)
    each(lambda d: copy(0, cs, cr, d, False).start())
    for name in names[EARLY:]:
        loads[name].start()

    loads["perm"].wait()
    loads["radiate"].wait()
    loads["shift"].wait()
    mixed = dot(vm["perm"][...], x_own[...]).astype(BF16)
    gp[...] = dot(mixed, vm["radiate"][...]).astype(BF16).astype(F32)
    shift = vm["shift"]
    quarter = own // 4

    def gather_up(source, level, rows):
        res, ims = [], []
        for t in range(tiles):
            lr_, li_ = slice(t * 128, t * 128 + 128), slice(half + t * 128, half + t * 128 + 128)
            re = jnp.zeros((rows, 128), F32)
            im = jnp.zeros((rows, 128), F32)
            for ab in range(4):
                tr, ti = shift[level, ab : ab + 1, lr_], shift[level, ab : ab + 1, li_]
                pr, pi = source[ab * rows : (ab + 1) * rows, lr_], source[ab * rows : (ab + 1) * rows, li_]
                re = re + (tr * pr - ti * pi)
                im = im + (tr * pi + ti * pr)
            res.append(re)
            ims.append(im)
        return jnp.concatenate(res + ims, axis=1)

    p1 = gather_up(gp, 0, quarter).astype(BF16)
    lown[0:quarter] = p1
    loads["split1"].wait()
    loads["split2"].wait()
    loads["send1"].wait()
    q2 = quarter // 4
    p2 = gather_up(dot(vm["split1"][...], p1), 1, q2).astype(BF16)
    lown[quarter : quarter + q2] = p2
    p3 = gather_up(dot(vm["split2"][...], p2), 2, 8)
    tail = lown.shape[0] - quarter - q2
    lown[quarter + q2 :] = jnp.concatenate([p3, jnp.zeros((tail - 8, feat), F32)], axis=0).astype(BF16)
    ls[...] = dot(vm["send1"][...], lown[...]).astype(BF16)
    each(lambda d: copy(1, ls, lr, d, False).start())

    loads["ext_own"].wait()
    loads["ext_got"].wait()
    each(lambda d: copy(0, cs, cr, d, True).wait_recv())
    ext = dot(vm["ext_own"][...], x_own[...]) + dot(vm["ext_got"][...], cr[...])
    ext_rows = ny + 8
    for c in range(w // 128):
        f0[c] = ext[:, c * 128 : c * 128 + 128].reshape(nx + 4, ext_rows, 128)
    ext = ext.astype(BF16)
    for c in range(0, feat // 128, 2):
        pat = dot(ext, vm["radiate"][:, c * 128 : c * 128 + 256]).astype(BF16).astype(F32)
        e0[c] = pat[:, :128].reshape(nx + 4, ext_rows, 128)
        e0[c + 1] = pat[:, 128:].reshape(nx + 4, ext_rows, 128)

    even16 = (lax.broadcasted_iota(jnp.int32, (1, ny, 128), 1) % 2) == 0
    pairs = nx // 2 + 2

    def shifted(k, _):
        for c in range(feat // 128):
            lanes = slice(c * 128, c * 128 + 128)
            for par in range(2):
                x = k * 2 + par
                for n, s in enumerate(SHIFTS):
                    v = e0[c, pl.ds(x, 1), 3 + s : 3 + s + ny, :]
                    if s == 3:
                        v = jnp.where(even16, v, e0[c, pl.ds(x, 1), 0:ny, :])
                    ps0[pl.ds(n * pairs + k, 1), par, :, lanes] = v.astype(BF16)
        return 0

    lax.fori_loop(0, pairs, shifted, 0)

    for n in range(3):
        for c in range(w // 128):
            ns[n, :, :, c * 128 : c * 128 + 128] = f0[c, 1 : nx + 3, 2 + n : 2 + n + ny, :].astype(BF16)
    loads["near_blocks"].wait()

    def near_part(n):
        columns = pl.ds(pl.multiple_of(n * (w // 2), w // 2), w // 2)
        views = [ns[k % 3, k // 3 : k // 3 + nx].reshape(own, w) for k in range(9)]
        near[:, columns] = dot(jnp.concatenate(views, axis=1), vm["near_blocks"][:, :, columns].reshape(9 * w, w // 2))

    loads["translate"].wait()
    translate = vm["translate"]

    def far(level, src, base, inc, lifted, beside=None):
        rows = src.shape[2]
        n_pairs = sizes[level][0] // 2
        npair = n_pairs + 2
        ni = min(4, n_pairs)
        even = (lax.broadcasted_iota(jnp.int32, (rows, 128), 0) % 2) == 0

        def step(it, _):
            if beside is None:
                piece(lax.rem(it, tiles), lax.div(it, tiles))
            else:
                beside(it)
                for k in range(tiles // 2):
                    for h in range(n_pairs // ni):
                        piece(it * (tiles // 2) + k, h)
            return 0

        def piece(t, h):
            rl = pl.ds(pl.multiple_of(t * 128, 128), 128)
            il = pl.ds(pl.multiple_of(half + t * 128, 128), 128)
            for a in range(2):
                re = jnp.zeros((ni, rows, 128), F32)
                im = jnp.zeros((ni, rows, 128), F32)
                narrow = src.dtype == BF16
                part, terms = None, 0
                for e in range(6):
                    dx = e - 2 - a
                    for n, s in enumerate(SHIFTS):
                        if max(abs(dx), abs(s)) < 2:
                            continue
                        k = (dx + 3) * 7 + s + 3
                        tr, ti = translate[k, level : level + 1, rl], translate[k, level : level + 1, il]
                        if s == 3:
                            m = (dx + 3) * 7
                            tr = jnp.where(even, tr, translate[m, level : level + 1, rl])
                            ti = jnp.where(even, ti, translate[m, level : level + 1, il])
                        at = pl.ds(base + n * npair + e // 2 + h * ni, ni)
                        pr, pi = src[at, e % 2, :, rl], src[at, e % 2, :, il]
                        if narrow:
                            tr = jnp.broadcast_to(tr, (rows, 128)).astype(BF16)
                            ti = jnp.broadcast_to(ti, (rows, 128)).astype(BF16)
                        more = (tr * pr - ti * pi, tr * pi + ti * pr)
                        part = more if part is None else (part[0] + more[0], part[1] + more[1])
                        terms += 1
                        if not narrow or terms % 3 == 0:
                            re = re + part[0].astype(F32)
                            im = im + part[1].astype(F32)
                            part = None
                at = pl.ds(h * ni, ni)
                if lifted is not None:
                    tr = jnp.where(even, shift[level, 2 * a : 2 * a + 1, rl], shift[level, 2 * a + 1 : 2 * a + 2, rl])
                    ti = jnp.where(even, shift[level, 2 * a : 2 * a + 1, il], shift[level, 2 * a + 1 : 2 * a + 2, il])
                    pr, pi = lifted[at, a, :, rl], lifted[at, a, :, il]
                    re = re + (tr * pr + ti * pi)
                    im = im + (tr * pi - ti * pr)
                inc[at, a, :, rl] = re.astype(inc.dtype)
                inc[at, a, :, il] = im.astype(inc.dtype)

        lax.fori_loop(0, tiles * (n_pairs // ni) if beside is None else 2, step, 0, unroll=beside is None)

    def lift(name, inc, dst):
        loads[name].wait()
        v = inc[...].reshape(-1, feat)
        hi = v.astype(BF16)
        rest = v - hi.astype(F32)
        mid = rest.astype(BF16)
        low = (rest - mid.astype(F32)).astype(BF16)
        dst[...] = dot(vm[name][...], jnp.concatenate([hi, mid, low], axis=0)).reshape(dst.shape)

    far(0, ps0, 0, far0, None, near_part)

    loads["up_own"].wait()
    loads["up_got"].wait()
    each(lambda d: copy(1, ls, lr, d, True).wait_recv())
    for c in range(0, feat, 256):
        v = dot(vm["up_own"][...], lown[:, c : c + 256]) + dot(vm["up_got"][...], lr[:, c : c + 256])
        psl[:, :, :, c : c + 256] = v.reshape(psl.shape[0], 2, 8, 256)

    bases, at = [], 0
    for a, _ in sizes[1:]:
        bases.append(at)
        at += 6 * (a // 2 + 2)
    far(3, psl, bases[2], inc3, None)
    lift("lift2", inc3, lift2)
    far(2, psl, bases[1], inc2, lift2)
    lift("lift1", inc2, lift1)
    far(1, psl, bases[0], inc1, lift1)
    lift("lift0", inc1, lift0)

    even = (lax.broadcasted_iota(jnp.int32, (ny, 128), 0) % 2) == 0

    def from_parents(t, _):
        rl = pl.ds(pl.multiple_of(t * 128, 128), 128)
        il = pl.ds(pl.multiple_of(half + t * 128, 128), 128)
        for a in range(2):
            tr = jnp.where(even, shift[0, 2 * a : 2 * a + 1, rl], shift[0, 2 * a + 1 : 2 * a + 2, rl])
            ti = jnp.where(even, shift[0, 2 * a : 2 * a + 1, il], shift[0, 2 * a + 1 : 2 * a + 2, il])
            pr, pi = lift0[:, a, :, rl], lift0[:, a, :, il]
            inc0[:, a, :, rl] = (far0[:, a, :, rl] + (tr * pr + ti * pi)).astype(BF16)
            inc0[:, a, :, il] = (far0[:, a, :, il] + (tr * pi - ti * pr)).astype(BF16)
        return 0

    lax.fori_loop(0, tiles, from_parents, 0, unroll=True)

    loads["receive"].wait()
    field = near[...] + dot(inc0[...].reshape(own, feat), vm["receive"][...])
    out_ref[...] = jnp.where(slot_of < cnt[...], field, 0.0).astype(BF16).reshape(nx, ny, w)

    each(lambda d: copy(0, cs, cr, d, False).wait_send())
    each(lambda d: copy(1, ls, lr, d, False).wait_send())


def hand_over(src, dst):
    dst[...] = src[...]


EARLY = 11
ORDER = ["counts", "ex", "ey", "currents", "send0", "perm", "radiate", "shift", "split1", "split2", "send1", "ext_own",
         "ext_got", "near_blocks", "up_own", "up_got", "translate", "lift2", "lift1", "lift0", "receive"]


def shards(currents, counts, radiate, receive, near_blocks, translate, shift):
    nx, ny, w = currents.shape
    feat = radiate.shape[1]
    consts, sizes = tables(nx, ny)
    ops = {k: jnp.asarray(v, BF16) for k, v in consts.items()}
    ops.update(currents=currents, counts=counts, radiate=radiate, receive=receive, near_blocks=near_blocks,
               translate=jnp.transpose(translate, (1, 0, 2)), shift=shift)
    args = [ops[k] for k in ORDER]
    own = nx * ny
    stack = consts["send1"].shape[1]
    rows = [max(8, b) for _, b in sizes]

    def level_buffer(level, dtype):
        return pltpu.VMEM((sizes[level][0] // 2, 2, rows[level], feat), dtype)

    scratch = [pltpu.VMEM(a.shape, a.dtype) for a in args]
    scratch += [
        pltpu.VMEM((own, w), BF16),
        pltpu.VMEM((ROWS, w), BF16),
        pltpu.VMEM((ROWS, w), BF16),
        pltpu.VMEM((own, feat), F32),
        pltpu.VMEM((stack, feat), BF16),
        pltpu.VMEM((ROWS, feat), BF16),
        pltpu.VMEM((ROWS, feat), BF16),
        pltpu.VMEM((feat // 128, nx + 4, ny + 8, 128), F32),
        pltpu.VMEM((w // 128, nx + 4, ny + 8, 128), F32),
        pltpu.VMEM((3, nx + 2, ny, w), BF16),
        pltpu.VMEM((6 * (nx // 2 + 2), 2, ny, feat), BF16),
        pltpu.VMEM((consts["up_own"].shape[0] // 16, 2, 8, feat), F32),
        level_buffer(0, F32), level_buffer(0, BF16), level_buffer(1, F32), level_buffer(2, F32), level_buffer(3, F32),
        level_buffer(0, F32), level_buffer(1, F32), level_buffer(2, F32),
        pltpu.VMEM((own, w), F32),
        pltpu.VMEM((own, w), F32),
        pltpu.SemaphoreType.DMA((len(args),)),
        pltpu.SemaphoreType.DMA((2, 8)),
        pltpu.SemaphoreType.DMA((2, 8)),
    ]
    field = pl.pallas_call(
        functools.partial(body, ORDER, sizes),
        out_shape=jax.ShapeDtypeStruct(currents.shape, BF16),
        in_specs=[pl.BlockSpec(memory_space=pl.ANY)] * len(args),
        out_specs=pl.BlockSpec(memory_space=pltpu.VMEM),
        scratch_shapes=scratch,
        compiler_params=pltpu.CompilerParams(
            collective_id=0, has_side_effects=True, vmem_limit_bytes=58 * 1024 * 1024
        ),
        cost_estimate=pl.CostEstimate(flops=3_000_000_000, bytes_accessed=12_000_000, transcendentals=0),
    )(*args)
    return pl.pallas_call(
        hand_over,
        out_shape=jax.ShapeDtypeStruct(field.shape, field.dtype),
        in_specs=[pl.BlockSpec(memory_space=pltpu.VMEM)],
        out_specs=pl.BlockSpec(memory_space=pltpu.VMEM),
    )(field)


def solution(mesh):
    return jax.shard_map(
        shards,
        mesh=mesh,
        in_specs=(P("row", "col", None), P("row", "col"), P(), P(), P(), P(), P()),
        out_specs=P("row", "col", None),
        check_vma=False,
    )
```
